128 devices in a mesh: seq: 8 (over x, core), exp: 16 (over y, z).
Axes of the slice: x: 4, y: 4, z: 4, core: 2. Of those that a mesh axis runs over, the one named last changes fastest.
Arguments:
- hidden: bfloat16 [16384, 2048], P(('seq', 'exp')), may hold values from -6 to 6
- cotangent: bfloat16 [16384, 2048], P(('seq', 'exp')), may hold values from -6 to 6
- norm_gain: float32 [2048], replicated, may hold values from 0.5 to 1.5
- router: bfloat16 [2048, 128], replicated, may hold values from -0.125 to 0.125
- w_gate: bfloat16 [128, 2048, 768], P(('seq', 'exp')), may hold values from -0.125 to 0.125
- w_up: bfloat16 [128, 2048, 768], P(('seq', 'exp')), may hold values from -0.125 to 0.125
- w_down: bfloat16 [128, 768, 2048], P(('seq', 'exp')), may hold values from -0.21875 to 0.21875
- expert_ids: int32 [16384, 8], P(('seq', 'exp')), may hold values from 0 to 127, all different within a row; in each aligned block of 128 rows (0 to 127, 128 to 255, ...) at most 10 rows name the same one
Outputs:
- d_hidden: bfloat16 [16384, 2048], P(('seq', 'exp'))
- d_gain: float32 [2048], replicated
- d_router: float32 [2048, 128], replicated
- d_wgate: bfloat16 [128, 2048, 768], P(('seq', 'exp'))
- d_wup: bfloat16 [128, 2048, 768], P(('seq', 'exp'))
- d_wdown: bfloat16 [128, 768, 2048], P(('seq', 'exp'))
The draws below stay inside these ranges and needn't reach their ends.
Inputs may be any that keep to these rules, and one draw needn't show every extreme that they name: `expert_ids`: each row names 8 different experts; among the 128 rows of one device no expert is named by more than 10 rows, a bound that some block reaches.
All inputs are finite; a program needn't handle non-finite values.
Results may differ from the reference program's by a relative error of at most 0.0083.
Values may be sent and summed in bfloat16 or wider, within the bound.
No kernel may reach another device: no remote copies, remote signals or barrier semaphores. Data moves between devices by JAX's collectives and lax.ppermute only.
A program may use at most 192 MiB of HBM per device.

```python
import math
import jax
import jax.numpy as jnp
import numpy as np
from jax import lax

D = 2048
F = 768
TOPK = 8
TOK_DEV = 128
EXPERTS = 128
TOKENS = 16384
CAP_SRC = 10
EXP_ROWS = 1024


def block_scale(stream_key, shape, cuts, smallest, largest):
    level, own = 1.0, jax.random.fold_in(stream_key, 6)
    for dim, blocks in cuts:
        draws = jnp.exp(jax.random.uniform(jax.random.fold_in(own, dim), (blocks,), jnp.float32, smallest / len(cuts), largest / len(cuts)))
        level = level * jnp.repeat(draws, shape[dim] // blocks).reshape([-1 if axis == dim else 1 for axis in range(len(shape))])
    return level


def deal_out(key, own, number, rows, amount, top, limit, slope):
    order = jax.random.permutation(key, amount)
    packed, ordinary = load_shares(amount, rows * top, limit, slope, True), load_shares(amount, rows * top, limit, slope, False)
    places = jnp.arange(amount)

    def named(tallies, turn):
        used = int((tallies > 0).sum())
        fixed = max(1, used // 4)
        moved = fixed + (places - fixed + turn * (used - fixed)) % max(1, amount - fixed)
        return jnp.zeros((amount,), jnp.int32).at[order[jnp.where(places < fixed, places, moved)]].set(jnp.asarray(tallies, jnp.int32))

    tallies = jnp.where(number % 4 == 0, named(packed, number // 4), named(ordinary, number - number // 4 - 1))
    mixed = jax.random.permutation(jax.random.fold_in(own, 3), amount)
    donor, receiver = mixed[0:amount // 2 * 2:2], mixed[1:amount // 2 * 2:2]
    slack = jnp.minimum(tallies[donor] - 1, limit - tallies[receiver]) // 2
    slack = jnp.where((donor == order[0]) | (receiver == order[0]) | (tallies[receiver] == 0), 0, jnp.maximum(slack, 0))
    moved = jax.random.randint(jax.random.fold_in(own, 4), (amount // 2,), 0, 1 << 20) % (slack + 1)
    tallies = tallies.at[donor].add(-moved).at[receiver].add(moved)
    labels = jnp.searchsorted(jnp.cumsum(tallies), jnp.arange(rows * top), side="right").astype(jnp.int32)
    table = labels.reshape(top, rows).T
    table = table[jax.random.permutation(jax.random.fold_in(own, 1), rows)]
    turn = jax.random.randint(jax.random.fold_in(own, 2), (rows, 1), 0, top)
    return jnp.take_along_axis(table, (jnp.arange(top)[None, :] + turn) % top, axis=1)


def load_shares(number_of, total, reach, lean, full):
    loads = [(1 << 20) // math.isqrt(standing ** lean) + 1 for standing in range(1, number_of + 1)]
    largest = reach if full else min(reach, max(-(-total // number_of), total * loads[0] // sum(loads)))
    least = 1 if total - largest >= number_of - 1 else 0
    counts, rest = [largest] + [least] * (number_of - 1), total - largest - least * (number_of - 1)
    while rest > 0:
        free = [i for i in range(1, number_of) if counts[i] < largest] or [i for i in range(1, number_of) if counts[i] < reach]
        mass, left = sum([loads[i] for i in free]), rest
        for i in free:
            more = min(reach - counts[i], max(1, left * loads[i] // mass), rest)
            counts[i] = counts[i] + more
            rest = rest - more
    return np.array(counts)


def centred(stream_key, dims, scale, most, split=(), held_as=jnp.bfloat16):
    drawn = jax.random.normal(stream_key, dims, jnp.float32) * scale
    if len(split) > 0:
        drawn = block_scale(stream_key, dims, split, -0.22, 0.18) * drawn
    return jnp.clip(drawn, min=-most, max=most).astype(held_as)


def setup_inputs(seed: int = 0) -> dict:
    seeds = jax.random.split(jax.random.key(seed), 9)
    hidden = centred(seeds[0], (TOKENS, D), 1.0, 6.0, ((0, 128),))
    cotangent = centred(seeds[1], (TOKENS, D), 1.0, 6.0, ((0, 128),))
    norm_gain = jnp.clip(1.0 + 0.1 * jax.random.normal(seeds[2], (D,), jnp.float32), 0.5, 1.5)
    router = centred(seeds[3], (D, EXPERTS), D ** -0.5, 0.125)
    w_gate = centred(seeds[4], (EXPERTS, D, F), D ** -0.5, 0.125, ((0, 128),))
    w_up = centred(seeds[5], (EXPERTS, D, F), D ** -0.5, 0.125, ((0, 128),))
    w_down = centred(seeds[6], (EXPERTS, F, D), F ** -0.5, 0.21875, ((0, 128),))
    expert_ids_keys = jax.random.split(jax.random.fold_in(seeds[7], 1), TOKENS // TOK_DEV)
    expert_ids_turns = jax.random.permutation(jax.random.fold_in(seeds[7], 3), TOKENS // TOK_DEV)
    expert_ids = jax.vmap(lambda own, number: deal_out(jax.random.fold_in(seeds[7], 2), own, number, TOK_DEV, EXPERTS, TOPK, CAP_SRC, 1))(expert_ids_keys, expert_ids_turns).reshape((TOKENS, TOPK))
    return dict(hidden=hidden, cotangent=cotangent, norm_gain=norm_gain, router=router, w_gate=w_gate, w_up=w_up, w_down=w_down, expert_ids=expert_ids)


norm_eps = 1e-06

def expert_backward(x_rows, cot_rows, gate_rows, weight_gate, weight_up, weight_down):
    pre_gate = jnp.dot(x_rows, weight_gate, preferred_element_type=jnp.float32)
    pre_up = jnp.dot(x_rows, weight_up, preferred_element_type=jnp.float32)
    sigm = jax.nn.sigmoid(pre_gate)
    act = (pre_gate * sigm * pre_up).astype(jnp.bfloat16)
    output = jnp.dot(act, weight_down, preferred_element_type=jnp.float32)
    gate_grad = lax.optimization_barrier(jnp.sum(cot_rows.astype(jnp.float32) * output, axis=1)).astype(jnp.bfloat16)
    gated = (gate_rows.astype(jnp.float32)[:, None] * cot_rows.astype(jnp.float32)).astype(jnp.bfloat16)
    d_act = jnp.dot(gated, weight_down.T, preferred_element_type=jnp.float32)
    grad_down = jnp.dot(act.T, gated, preferred_element_type=jnp.float32).astype(jnp.bfloat16)
    grad_pre_gate = (d_act * pre_up * sigm * (1.0 + pre_gate * (1.0 - sigm))).astype(jnp.bfloat16)
    grad_pre_up = (d_act * pre_gate * sigm).astype(jnp.bfloat16)
    grad_gate = jnp.dot(x_rows.T, grad_pre_gate, preferred_element_type=jnp.float32).astype(jnp.bfloat16)
    grad_up = jnp.dot(x_rows.T, grad_pre_up, preferred_element_type=jnp.float32).astype(jnp.bfloat16)
    grad_x = (jnp.dot(grad_pre_gate, weight_gate.T, preferred_element_type=jnp.float32) + jnp.dot(grad_pre_up, weight_up.T, preferred_element_type=jnp.float32)).astype(jnp.bfloat16)
    return (grad_x, gate_grad, grad_gate, grad_up, grad_down)

def reference(hidden, cotangent, norm_gain, router, w_gate, w_up, w_down, expert_ids):
    token_count, model_width = hidden.shape
    top_count = expert_ids.shape[1]
    expert_count = router.shape[1]
    slot_rows = EXP_ROWS
    hidden_f = hidden.astype(jnp.float32)
    scale_r = lax.rsqrt(lax.optimization_barrier(jnp.mean(hidden_f * hidden_f, axis=-1, keepdims=True)) + norm_eps)
    normed = (hidden_f * scale_r * norm_gain).astype(jnp.bfloat16)
    logits = jnp.dot(normed, router, preferred_element_type=jnp.float32)
    picked = jnp.take_along_axis(logits, expert_ids, axis=1)
    weights = jnp.exp(picked)
    gates = weights / lax.optimization_barrier(jnp.sum(weights, axis=1, keepdims=True))
    assign_count = token_count * top_count
    flat_ids = expert_ids.reshape(-1)
    one_hot = (flat_ids[:, None] == jnp.arange(expert_count, dtype=jnp.int32)[None, :]).astype(jnp.int32)
    position = lax.optimization_barrier(jnp.sum((jnp.cumsum(one_hot, axis=0) - one_hot) * one_hot, axis=1)).astype(jnp.int32)
    kept = position < slot_rows
    target = jnp.where(kept, flat_ids * slot_rows + position, expert_count * slot_rows).astype(jnp.int32)
    table = jnp.full((expert_count * slot_rows + 1,), assign_count, jnp.int32)
    table = table.at[target].set(jnp.arange(assign_count, dtype=jnp.int32))
    table = table[:expert_count * slot_rows].reshape(expert_count, slot_rows)
    normed_pad = jnp.concatenate([normed, jnp.zeros((1, model_width), jnp.bfloat16)], axis=0)
    cot_pad = jnp.concatenate([cotangent, jnp.zeros((1, model_width), jnp.bfloat16)], axis=0)
    gate_pad = jnp.concatenate([gates.reshape(-1).astype(jnp.bfloat16), jnp.zeros((1,), jnp.bfloat16)])

    def one_expert(carry, inputs):
        grad_acc, dgate_acc = carry
        index_rows, weight_gate, weight_up, weight_down = inputs
        token_rows = index_rows // top_count
        grad_x, gate_grad, grad_gate, grad_up, grad_down = expert_backward(normed_pad[token_rows], cot_pad[token_rows], gate_pad[index_rows], weight_gate, weight_up, weight_down)
        grad_acc = grad_acc.at[token_rows].add(grad_x.astype(jnp.float32), mode='drop')
        dgate_acc = dgate_acc.at[index_rows].add(gate_grad.astype(jnp.float32), mode='drop')
        return ((grad_acc, dgate_acc), (grad_gate, grad_up, grad_down))
    start = (jnp.zeros((token_count, model_width), jnp.float32), jnp.zeros((assign_count,), jnp.float32))
    (grad_acc, dgate_acc), (d_wgate, d_wup, d_wdown) = lax.scan(one_expert, start, (table, w_gate, w_up, w_down))
    dgate = dgate_acc.reshape(token_count, top_count)
    dsel = gates * (dgate - lax.optimization_barrier(jnp.sum(gates * dgate, axis=1, keepdims=True)))
    match = expert_ids[:, :, None] == jnp.arange(expert_count, dtype=jnp.int32)[None, None, :]
    dlogits = lax.optimization_barrier(jnp.sum(jnp.where(match, dsel[:, :, None], 0.0), axis=1)).astype(jnp.bfloat16)
    d_router = jnp.dot(normed.T, dlogits, preferred_element_type=jnp.float32)
    dnormed = grad_acc + jnp.dot(dlogits, router.T, preferred_element_type=jnp.float32)
    d_gain = lax.optimization_barrier(jnp.sum(dnormed * hidden_f * scale_r, axis=0))
    gained = norm_gain * dnormed
    d_hidden = (cotangent.astype(jnp.float32) + scale_r * gained - hidden_f * scale_r ** 3 * lax.optimization_barrier(jnp.mean(gained * hidden_f, axis=-1, keepdims=True))).astype(jnp.bfloat16)
    return (d_hidden, d_gain, d_router, d_wgate, d_wup, d_wdown)
```

```python
import functools

import jax
import jax.numpy as jnp
from jax import lax
from jax.experimental import pallas as pl
from jax.experimental.pallas import tpu as pltpu
from jax.sharding import PartitionSpec as P

norm_eps = 1e-06
HI = 8
SUB = 8
MSG = 128
AXES = ("seq", "exp")
bf16, f32 = jnp.bfloat16, jnp.float32
VMEM_LIMIT = 56 * 1024 * 1024


def params(**kw):
    return pltpu.CompilerParams(vmem_limit_bytes=VMEM_LIMIT, **kw)


def whole(shape):
    return pl.BlockSpec(shape, lambda *_: (0,) * len(shape))


def iota(shape, dim):
    return lax.broadcasted_iota(jnp.int32, shape, dim)


def mm(a, b):
    return jnp.dot(a, b, preferred_element_type=f32)


def mm_nt(a, b):
    return lax.dot_general(a, b, (((1,), (1,)), ((), ())), preferred_element_type=f32)


def mm_tn(a, b):
    return lax.dot_general(a, b, (((0,), (0,)), ((), ())), preferred_element_type=f32)


def exchange(x):
    return lax.all_to_all(x, AXES, split_axis=0, concat_axis=0, tiled=True)


def front_kernel(hid_ref, cot_ref, gain_ref, ids_ref, s1_ref, normed_ref, slot_ref, slot_t_ref, nc, p8):
    step = pl.program_id(0)
    tokens, width = hid_ref.shape
    experts = slot_ref.shape[1]
    tile = nc.shape[2]

    @pl.when(step == 0)
    def _():
        h = hid_ref[...].astype(f32)
        scale = lax.rsqrt(jnp.mean(h * h, axis=1, keepdims=True) + norm_eps)
        normed = (h * scale * gain_ref[...]).astype(bf16)
        normed_ref[...] = normed
        for j in range(width // tile):
            nc[j] = normed[:, j * tile : (j + 1) * tile]
            nc[width // tile + j] = cot_ref[:, j * tile : (j + 1) * tile]
        ids = ids_ref[...]
        lane = iota((tokens, experts), 1)
        member = jnp.zeros((tokens, experts), f32)
        for k in range(ids.shape[1]):
            member += jnp.where(ids[:, k : k + 1] == lane, 1.0, 0.0)
        lower = jnp.where(iota((tokens, tokens), 1) < iota((tokens, tokens), 0), 1.0, 0.0)
        position = mm(lower.astype(bf16), member.astype(bf16))
        slot = jnp.where(member > 0.0, position, 99.0)
        slot_ref[...] = slot
        slot_t = slot.T
        slot_t_ref[...] = slot_t
        which = iota((experts, HI, tokens), 1).astype(f32)
        chosen = jnp.where(slot_t[:, None, :] == which, 1.0, 0.0)
        p8[...] = chosen.reshape(experts * HI, tokens).astype(bf16)

    s1_ref[...] = mm(p8[...], nc[step]).astype(bf16)


def front(hidden, cotangent, gain, ids, experts):
    tokens, width = hidden.shape
    tile = min(512, width)
    steps = 2 * width // tile
    return pl.pallas_call(
        front_kernel,
        grid=(steps,),
        in_specs=[whole((tokens, width)), whole((tokens, width)), whole((1, width)), whole(ids.shape)],
        out_specs=[
            pl.BlockSpec((experts * HI, tile), lambda i: (0, i)),
            whole((tokens, width)),
            whole((tokens, experts)),
            whole((experts, tokens)),
        ],
        out_shape=[
            jax.ShapeDtypeStruct((experts * HI, 2 * width), bf16),
            jax.ShapeDtypeStruct((tokens, width), bf16),
            jax.ShapeDtypeStruct((tokens, experts), f32),
            jax.ShapeDtypeStruct((experts, tokens), f32),
        ],
        scratch_shapes=[pltpu.VMEM((steps, tokens, tile), bf16), pltpu.VMEM((experts * HI, tokens), bf16)],
        compiler_params=params(),
        cost_estimate=pl.CostEstimate(flops=4 * experts * HI * tokens * width, bytes_accessed=10_000_000, transcendentals=tokens),
    )(hidden, cotangent, gain, ids)


def second_kernel(normed_ref, cot_ref, slot_ref, slot_t_ref, router_ref, gates_ref, s2_ref):
    tokens, width = normed_ref.shape
    experts = slot_ref.shape[1]
    half = width // 2
    logits = mm(normed_ref[...], router_ref[...])
    weights = jnp.where(slot_ref[...] < 50.0, jnp.exp(logits), 0.0)
    gates = weights / jnp.sum(weights, axis=1, keepdims=True)
    gates_ref[...] = gates
    slot_t = slot_t_ref[...]
    gates_t = gates.T
    lane = iota((experts, MSG), 1)
    message = jnp.where(lane == 10, jnp.sum(jnp.where(slot_t < 50.0, 1.0, 0.0), axis=1, keepdims=True), 0.0)
    for s in range(10):
        message = message + jnp.where(
            lane == s, jnp.sum(jnp.where(slot_t == s, gates_t, 0.0), axis=1, keepdims=True), 0.0
        )
    sub = iota((experts, SUB, MSG), 1)
    spread = jnp.where(sub == 0, message[:, None, :], 0.0).reshape(experts * SUB, MSG)
    s2_ref[:, half:] = spread.astype(bf16)
    row = iota((experts, SUB, tokens), 1)
    chosen = jnp.where(slot_t[:, None, :] == (HI + row // 4).astype(f32), 1.0, 0.0)
    total = None
    for j in range(4):
        pick = jnp.where(row % 4 == j, chosen, 0.0).reshape(experts * SUB, tokens).astype(bf16)
        source = normed_ref if j < 2 else cot_ref
        term = mm(pick, source[:, (j % 2) * half : (j % 2 + 1) * half])
        total = term if total is None else total + term
    s2_ref[:, :half] = total.astype(bf16)


def second(normed, cotangent, slot, slot_t, router):
    tokens, width = normed.shape
    experts = slot.shape[1]
    return pl.pallas_call(
        second_kernel,
        out_shape=[
            jax.ShapeDtypeStruct((tokens, experts), f32),
            jax.ShapeDtypeStruct((experts * SUB, width // 2 + MSG), bf16),
        ],
        compiler_params=params(),
        cost_estimate=pl.CostEstimate(flops=4 * experts * SUB * tokens * width, bytes_accessed=4_000_000, transcendentals=tokens * experts),
    )(normed, cotangent, slot, slot_t, router)


def expert_rows(x, c, wg_ref, wu_ref, wd_ref):
    a = mm(x, wg_ref[...])
    b = mm(x, wu_ref[...])
    u = mm_nt(c, wd_ref[...])
    s = jax.nn.sigmoid(a)
    act = (a * s * b).astype(bf16)
    q = jnp.sum(act.astype(f32) * u, axis=1, keepdims=True)
    da = (u * b * s * (1.0 + a * (1.0 - s))).astype(bf16)
    db = (u * a * s).astype(bf16)
    return act, q, da, db


def rows_kernel(x_ref, c_ref, wg_ref, wu_ref, wd_ref, act_ref, da_ref, db_ref, q_ref, dx_ref):
    act, q, da, db = expert_rows(x_ref[...], c_ref[...], wg_ref, wu_ref, wd_ref)
    act_ref[...] = act
    da_ref[...] = da
    db_ref[...] = db
    sources = q_ref.shape[0]
    lane, which = iota((sources, HI, MSG), 2), iota((sources, HI, MSG), 1)
    q_ref[...] = jnp.sum(jnp.where(lane == which, q.reshape(sources, HI, 1), 0.0), axis=1)
    dx_ref[...] = (mm_nt(da, wg_ref[...]) + mm_nt(db, wu_ref[...])).astype(bf16)


def rows(r1, wg, wu, wd):
    total, both = r1.shape
    width, hid = wg.shape
    block = min(256, total)
    one = pl.BlockSpec((block, hid), lambda i: (i, 0))
    return pl.pallas_call(
        rows_kernel,
        grid=(total // block,),
        in_specs=[
            pl.BlockSpec((block, width), lambda i: (i, 0)),
            pl.BlockSpec((block, width), lambda i: (i, 1)),
            whole(wg.shape),
            whole(wu.shape),
            whole(wd.shape),
        ],
        out_specs=[one, one, one, pl.BlockSpec((block // HI, MSG), lambda i: (i, 0)), pl.BlockSpec((block, width), lambda i: (i, 0))],
        out_shape=[jax.ShapeDtypeStruct((total, hid), bf16)] * 3
        + [
            jax.ShapeDtypeStruct((total // HI, MSG), f32),
            jax.ShapeDtypeStruct((total, width + width // 2), bf16),
        ],
        compiler_params=params(),
        cost_estimate=pl.CostEstimate(flops=10 * total * width * hid, bytes_accessed=30_000_000, transcendentals=total * hid),
    )(r1, r1, wg, wu, wd)


def tail_kernel(limit, r2_ref, q8_ref, wg_ref, wu_ref, wd_ref, xc_ref, act_ref, da_ref, db_ref, msg_ref, scale_ref):
    sources = q8_ref.shape[0]
    width, hid = wg_ref.shape
    half = width // 2
    chunk = min(32, sources)
    out_rows, in_rows = 2 * chunk, SUB * chunk
    index, column = iota((4 * out_rows, in_rows), 0), iota((4 * out_rows, in_rows), 1)
    pick = jnp.where(column == 4 * (index % out_rows) + index // out_rows, 1.0, 0.0).astype(bf16)
    for j in range(sources // chunk):
        part = mm(pick, r2_ref[j * in_rows : (j + 1) * in_rows, :half]).astype(bf16)
        for quarter in range(4):
            xc_ref[j * out_rows : (j + 1) * out_rows, quarter * half : (quarter + 1) * half] = part[
                quarter * out_rows : (quarter + 1) * out_rows
            ]
    act, q, da, db = expert_rows(xc_ref[:, :width], xc_ref[:, width:], wg_ref, wu_ref, wd_ref)
    act_ref[...] = act
    da_ref[...] = da
    db_ref[...] = db
    total = 2 * sources
    parity = iota((total, MSG), 0) % 2
    spread = jnp.where(iota((total, MSG), 1) == HI + parity, q, 0.0).astype(bf16)
    gather = jnp.where(iota((sources, total), 1) // 2 == iota((sources, total), 0), 1.0, 0.0).astype(bf16)
    q_all = q8_ref[...].astype(bf16).astype(f32) + mm(gather, spread)
    meta = jnp.sum(r2_ref[:, half:].astype(f32).reshape(sources, SUB, MSG), axis=1)
    lane = iota((sources, MSG), 1)
    count = jnp.sum(jnp.where(lane == 10, meta, 0.0), axis=1, keepdims=True)
    lower = jnp.where(iota((sources, sources), 1) < iota((sources, sources), 0), 1.0, 0.0).astype(bf16)
    offset = mm(lower, jnp.broadcast_to(count, (sources, MSG)).astype(bf16))
    slot = jnp.where(lane < 10, lane, lane - 10).astype(f32)
    kept = (slot < count) & (offset + slot < limit) & (lane < 20)
    msg_ref[...] = jnp.where(kept, jnp.where(lane < 10, q_all, 1.0), 0.0)
    scale_ref[...] = jnp.where(kept & (lane < 10), meta, 0.0).astype(bf16)


def tail(r2, q8, wg, wu, wd, limit):
    sources = q8.shape[0]
    width, hid = wg.shape
    return pl.pallas_call(
        functools.partial(tail_kernel, float(limit)),
        out_shape=[jax.ShapeDtypeStruct((2 * sources, 2 * width), bf16)]
        + [jax.ShapeDtypeStruct((2 * sources, hid), bf16)] * 3
        + [jax.ShapeDtypeStruct((sources, MSG), f32), jax.ShapeDtypeStruct((sources, MSG), bf16)],
        compiler_params=params(),
        cost_estimate=pl.CostEstimate(flops=12 * sources * width * hid, bytes_accessed=16_000_000, transcendentals=2 * sources * hid),
    )(r2, q8, wg, wu, wd)


def tail_dx_kernel(da_ref, db_ref, wg_ref, wu_ref, dx_ref):
    dx_ref[...] = (mm_nt(da_ref[...], wg_ref[...]) + mm_nt(db_ref[...], wu_ref[...])).astype(bf16)


def tail_dx(da, db, wg, wu):
    return pl.pallas_call(
        tail_dx_kernel,
        out_shape=jax.ShapeDtypeStruct((da.shape[0], wg.shape[0]), bf16),
        compiler_params=params(),
        cost_estimate=pl.CostEstimate(flops=4 * da.shape[0] * wg.size, bytes_accessed=8_000_000, transcendentals=0),
    )(da, db, wg, wu)


def column_of(table):
    sources = table.shape[0]
    lane, which = iota((sources, HI, MSG), 2), iota((sources, HI, MSG), 1)
    spread = jnp.where(lane == which, table[:, None, :], 0.0)
    return jnp.sum(spread.reshape(sources * HI, MSG), axis=1, keepdims=True)


def tail_column_of(table):
    sources = table.shape[0]
    total = 2 * sources
    scatter = jnp.where(iota((total, sources), 0) // 2 == iota((total, sources), 1), 1.0, 0.0).astype(bf16)
    lane = HI + iota((total, MSG), 0) % 2
    return jnp.sum(jnp.where(iota((total, MSG), 1) == lane, mm(scatter, table), 0.0), axis=1, keepdims=True)


def weights_kernel(x_ref, c_ref, x2_ref, c2_ref, act_ref, da_ref, db_ref, act2_ref, da2_ref, db2_ref, scale_ref, wg_ref, wu_ref, dwg_ref, dwu_ref, dwd_ref, part_ref, act_s, da_s, db_s):
    main = act_ref.shape[0]

    @pl.when(pl.program_id(0) == 0)
    def _():
        table = scale_ref[...]
        column, tail_column = column_of(table.astype(f32)), tail_column_of(table)
        for source, source2, target in ((act_ref, act2_ref, act_s), (da_ref, da2_ref, da_s), (db_ref, db2_ref, db_s)):
            target[:main] = (source[...].astype(f32) * column).astype(bf16)
            target[main:] = (source2[...].astype(f32) * tail_column).astype(bf16)

    def both(first, second, scaled):
        return mm_tn(first, scaled[:main]) + mm_tn(second, scaled[main:])

    dwg = both(x_ref[...], x2_ref[...], da_s)
    dwu = both(x_ref[...], x2_ref[...], db_s)
    dwg_ref[...] = dwg.astype(bf16)
    dwu_ref[...] = dwu.astype(bf16)
    dwd_ref[...] = (mm_tn(act_s[:main], c_ref[...]) + mm_tn(act_s[main:], c2_ref[...])).astype(bf16)
    product = dwg * wg_ref[...].astype(f32) + dwu * wu_ref[...].astype(f32)
    folded = product[:, :MSG]
    for j in range(1, product.shape[1] // MSG):
        folded = folded + product[:, j * MSG : (j + 1) * MSG]
    part_ref[...] = jnp.broadcast_to(jnp.sum(folded.T, axis=0, keepdims=True), part_ref.shape)


def weight_grads(r1, xc2, acts, acts2, scale, wg, wu):
    main, tail_rows = r1.shape[0], xc2.shape[0]
    width, hid = wg.shape
    tile = min(256, width)
    steps = width // tile
    return pl.pallas_call(
        weights_kernel,
        grid=(steps,),
        in_specs=[
            pl.BlockSpec((main, tile), lambda i: (0, i)),
            pl.BlockSpec((main, tile), lambda i: (0, i + steps)),
            pl.BlockSpec((tail_rows, tile), lambda i: (0, i)),
            pl.BlockSpec((tail_rows, tile), lambda i: (0, i + steps)),
        ]
        + [whole((main, hid))] * 3
        + [whole((tail_rows, hid))] * 3
        + [whole(scale.shape)]
        + [pl.BlockSpec((tile, hid), lambda i: (i, 0))] * 2,
        out_specs=[
            pl.BlockSpec((tile, hid), lambda i: (i, 0)),
            pl.BlockSpec((tile, hid), lambda i: (i, 0)),
            pl.BlockSpec((hid, tile), lambda i: (0, i)),
            pl.BlockSpec((8, tile), lambda i: (0, i)),
        ],
        out_shape=[
            jax.ShapeDtypeStruct((width, hid), bf16),
            jax.ShapeDtypeStruct((width, hid), bf16),
            jax.ShapeDtypeStruct((hid, width), bf16),
            jax.ShapeDtypeStruct((8, width), f32),
        ],
        scratch_shapes=[pltpu.VMEM((main + tail_rows, hid), bf16)] * 3,
        compiler_params=params(),
        cost_estimate=pl.CostEstimate(flops=6 * (main + tail_rows) * width * hid, bytes_accessed=36_000_000, transcendentals=0),
    )(r1, r1, xc2, xc2, *acts, *acts2, scale, wg, wu)


def home_kernel(q_ref, slot_ref, gates_ref, dl_ref, gk_t_ref, msg_ref):
    experts = q_ref.shape[0]
    q_t = q_ref[...].T
    slot, gates = slot_ref[...], gates_ref[...]
    dgate = jnp.zeros_like(gates)
    kept = jnp.zeros_like(gates)
    for s in range(10):
        here = slot == s
        dgate = dgate + jnp.where(here, q_t[s : s + 1, :], 0.0)
        kept = kept + jnp.where(here, q_t[10 + s : 11 + s, :], 0.0)
    dsel = gates * (dgate - jnp.sum(gates * dgate, axis=1, keepdims=True))
    dl = dsel.astype(bf16)
    dl_ref[...] = dl
    gk_t_ref[...] = (gates.astype(bf16).astype(f32) * kept).T
    dl = dl.astype(f32)
    lane = iota((MSG, experts), 0)
    out = jnp.zeros((MSG, experts), f32)
    for s in range(10):
        out = out + jnp.where(lane == s, jnp.sum(jnp.where(slot == s, dl, 0.0), axis=0, keepdims=True), 0.0)
    msg_ref[...] = out.T


def home(q, slot, gates):
    tokens, experts = slot.shape
    return pl.pallas_call(
        home_kernel,
        out_shape=[
            jax.ShapeDtypeStruct((tokens, experts), bf16),
            jax.ShapeDtypeStruct((experts, tokens), f32),
            jax.ShapeDtypeStruct((experts, MSG), f32),
        ],
        compiler_params=params(),
        cost_estimate=pl.CostEstimate(flops=40 * tokens * experts, bytes_accessed=400_000, transcendentals=0),
    )(q, slot, gates)


def narrow_kernel(ds_ref, x_ref, x2_ref, dx2_ref, part_ref, _, out_ref):
    sources = ds_ref.shape[0]
    width = x_ref.shape[1]
    half = width // 2
    table = ds_ref[...]
    column = jnp.broadcast_to(column_of(table), (sources * HI, MSG)).astype(bf16)
    tail_column = jnp.broadcast_to(tail_column_of(table.astype(bf16)), (2 * sources, MSG)).astype(bf16)
    dr = (mm_tn(column, x_ref[...]) + mm_tn(tail_column, x2_ref[...]))[0:1]
    part = part_ref[0:1, :]
    chunk = min(32, sources)
    n_rows = SUB * chunk
    row, col = iota((n_rows, 4 * chunk), 0), iota((n_rows, 4 * chunk), 1)
    sub = row % SUB
    source_row = 2 * (row // SUB) + sub // 2 + (sub % 2) * 2 * chunk
    pick = jnp.where((sub < 4) & (col == source_row), 1.0, 0.0).astype(bf16)
    sub = iota((n_rows, half), 0) % SUB
    fixed = jnp.where(sub == 4, dr[:, :half], 0.0)
    fixed = jnp.where(sub == 5, dr[:, half:], fixed)
    fixed = jnp.where(sub == 6, part[:, :half], fixed)
    fixed = jnp.where(sub == 7, part[:, half:], fixed)
    for j in range(sources // chunk):
        dx2 = dx2_ref[j * 2 * chunk : (j + 1) * 2 * chunk, :]
        halves = jnp.concatenate([dx2[:, :half], dx2[:, half:]], axis=0)
        out_ref[j * n_rows : (j + 1) * n_rows, :] = (mm(pick, halves) + fixed).astype(bf16)


def narrow(ds, r1, xc2, dx2, part, back):
    sources = ds.shape[0]
    width = dx2.shape[1]
    half = width // 2
    return pl.pallas_call(
        narrow_kernel,
        grid=(1,),
        in_specs=[
            whole(ds.shape),
            pl.BlockSpec((sources * HI, width), lambda i: (0, 0)),
            pl.BlockSpec((2 * sources, width), lambda i: (0, 0)),
            whole(dx2.shape),
            whole(part.shape),
            pl.BlockSpec(memory_space=pl.ANY),
        ],
        out_specs=pl.BlockSpec((sources * SUB, half), lambda i: (0, 2)),
        out_shape=jax.ShapeDtypeStruct(back.shape, bf16),
        input_output_aliases={5: 0},
        compiler_params=params(),
        cost_estimate=pl.CostEstimate(flops=3 * sources * HI * MSG * width, bytes_accessed=9_000_000, transcendentals=0),
    )(ds, r1, xc2, dx2, part, back)


def final_kernel(dx_ref, ext_ref, slot_t_ref, gk_t_ref, dl_ref, router_t_ref, gain_ref, hid_ref, cot_ref, dh_ref, dgain_ref, drouter_ref, total, columns, gains):
    step, last = pl.program_id(0), pl.num_programs(0) - 1
    chunk, tokens = slot_t_ref.shape
    n_rows = chunk * SUB
    width = hid_ref.shape[1]
    half = width // 2
    slot, gk = slot_t_ref[...][:, None, :], gk_t_ref[...][:, None, :]
    which = iota((chunk, SUB, tokens), 1)

    def weights(mask):
        return jnp.where(mask, gk, 0.0).reshape(n_rows, tokens).astype(bf16)

    ext = ext_ref[...]
    main = mm_tn(weights(slot == which.astype(f32)), dx_ref[...])
    in_tail = (which < 4) & (slot == (HI + which // 2).astype(f32))
    low = mm_tn(weights(in_tail & (which % 2 == 0)), ext)
    high = mm_tn(weights(in_tail & (which % 2 == 1)), ext)
    row, col = iota((chunk, n_rows), 0), iota((chunk, n_rows), 1)

    def every(sub):
        return mm(jnp.where(col == row * SUB + sub, 1.0, 0.0).astype(bf16), ext)

    begin = pl.multiple_of(step * chunk, chunk)
    for side, offset in ((0, 0), (1, half)):
        router_rows = every(4 + side)
        columns[pl.ds(begin, chunk), offset : offset + half] = router_rows
        gain_rows = every(6 + side) + router_rows * router_t_ref[:, offset : offset + half].astype(f32)
        gain_sum = jnp.sum(gain_rows, axis=0, keepdims=True)
        tail_part = high if side else low

        @pl.when(step == 0)
        def _():
            gains[:, offset : offset + half] = gain_sum
            total[:, offset : offset + half] = main[:, offset : offset + half] + tail_part

        @pl.when(step > 0)
        def _():
            gains[:, offset : offset + half] += gain_sum
            total[:, offset : offset + half] += main[:, offset : offset + half] + tail_part

    total[...] += mm(dl_ref[...], router_t_ref[...])

    @pl.when(step == last)
    def _():
        gain = gain_ref[...]
        h = hid_ref[...].astype(f32)
        scale = lax.rsqrt(jnp.mean(h * h, axis=1, keepdims=True) + norm_eps)
        gained = gain * total[...]
        mean = jnp.mean(gained * h, axis=1, keepdims=True)
        dh_ref[...] = (cot_ref[...].astype(f32) + scale * gained - h * (scale * scale * scale) * mean).astype(bf16)
        dgain_ref[...] = gains[...] / gain
        drouter_ref[...] = columns[...].T


def final(rd, slot_t, gk_t, dl, router_t, gain, hidden, cotangent):
    experts, tokens = slot_t.shape
    width = hidden.shape[1]
    half = width // 2
    chunk = min(32, experts)
    steps = experts // chunk
    return pl.pallas_call(
        final_kernel,
        grid=(steps,),
        in_specs=[
            pl.BlockSpec((chunk * SUB, width), lambda i: (i, 0)),
            pl.BlockSpec((chunk * SUB, half), lambda i: (i, 2)),
            pl.BlockSpec((chunk, tokens), lambda i: (i, 0)),
            pl.BlockSpec((chunk, tokens), lambda i: (i, 0)),
            pl.BlockSpec((None, tokens, chunk), lambda i: (i, 0, 0)),
            pl.BlockSpec((chunk, width), lambda i: (i, 0)),
            whole((1, width)),
            whole((tokens, width)),
            whole((tokens, width)),
        ],
        out_specs=[whole((tokens, width)), whole((1, width)), whole((width, experts))],
        out_shape=[
            jax.ShapeDtypeStruct((tokens, width), bf16),
            jax.ShapeDtypeStruct((1, width), f32),
            jax.ShapeDtypeStruct((width, experts), f32),
        ],
        scratch_shapes=[pltpu.VMEM((tokens, width), f32), pltpu.VMEM((experts, width), f32), pltpu.VMEM((1, width), f32)],
        compiler_params=params(),
        cost_estimate=pl.CostEstimate(flops=4 * experts * SUB * tokens * width, bytes_accessed=9_000_000, transcendentals=tokens),
    )(rd, rd, slot_t, gk_t, dl, router_t, gain, hidden, cotangent)


def on_device(hidden, cotangent, norm_gain, router, w_gate, w_up, w_down, expert_ids):
    tokens, width = hidden.shape
    top = expert_ids.shape[1]
    experts = router.shape[1]
    half = width // 2
    limit = tokens * top
    gain = norm_gain.reshape(1, width)
    wg, wu, wd = w_gate[0], w_up[0], w_down[0]

    s1, normed, slot, slot_t = front(hidden, cotangent, gain, expert_ids, experts)
    r1 = exchange(s1.reshape(experts, HI, 2 * width)).reshape(experts * HI, 2 * width)
    gates, s2 = second(normed, cotangent, slot, slot_t, router)
    r2 = exchange(s2.reshape(experts, SUB, half + MSG)).reshape(experts * SUB, half + MSG)
    act, da, db, q8, back = rows(r1, wg, wu, wd)
    xc2, act2, da2, db2, q_msg, scale = tail(r2, q8, wg, wu, wd, limit)
    q_home = exchange(q_msg.reshape(experts, 1, MSG)).reshape(experts, MSG)
    dx2 = tail_dx(da2, db2, wg, wu)
    d_wgate, d_wup, d_wdown, part = weight_grads(r1, xc2, (act, da, db), (act2, da2, db2), scale, wg, wu)
    dl, gk_t, ds_msg = home(q_home, slot, gates)
    ds = exchange(ds_msg.reshape(experts, 1, MSG)).reshape(experts, MSG)
    back = narrow(ds, r1, xc2, dx2, part, back)
    rd = exchange(back.reshape(experts, HI, width + half)).reshape(experts * HI, width + half)
    chunk = min(32, experts)
    dl = dl.reshape(tokens, experts // chunk, chunk).transpose(1, 0, 2)
    d_hidden, d_gain, d_router = final(rd, slot_t, gk_t, dl, router.T, gain, hidden, cotangent)
    return (d_hidden, d_gain.reshape(width), d_router, d_wgate[None], d_wup[None], d_wdown[None])


def solution(mesh):
    rows_spec, stack_spec = P(AXES, None), P(AXES, None, None)
    in_specs = (rows_spec, rows_spec, P(), P(), stack_spec, stack_spec, stack_spec, rows_spec)
    out_specs = (rows_spec, P(), P(), stack_spec, stack_spec, stack_spec)
    return jax.shard_map(on_device, mesh=mesh, in_specs=in_specs, out_specs=out_specs, check_vma=False)
```

```python
import functools

import jax
import jax.numpy as jnp
from jax import lax
from jax.experimental import pallas as pl
from jax.experimental.pallas import tpu as pltpu
from jax.sharding import PartitionSpec as P

norm_eps = 1e-06
HI = 8
SUB = 8
MSG = 128
AXES = ("seq", "exp")
bf16, f32 = jnp.bfloat16, jnp.float32


def params():
    return pltpu.CompilerParams(vmem_limit_bytes=60 * 1024 * 1024)


def whole(shape, **kw):
    return pl.BlockSpec(shape, lambda *_: (0,) * len(shape), **kw)


def iota(shape, dim):
    return lax.broadcasted_iota(jnp.int32, shape, dim)


def mm(a, b):
    return jnp.dot(a, b, preferred_element_type=f32)


def mm_nt(a, b):
    return lax.dot_general(a, b, (((1,), (1,)), ((), ())), preferred_element_type=f32)


def mm_tn(a, b):
    return lax.dot_general(a, b, (((0,), (0,)), ((), ())), preferred_element_type=f32)


def exchange(x):
    return lax.all_to_all(x, AXES, split_axis=0, concat_axis=0, tiled=True)


def front_kernel(hid_ref, cot_ref, gain_ref, ids_ref, s1_ref, normed_ref, slot_ref, slot_t_ref, nc, p8):
    step = pl.program_id(0)
    tokens, width = hid_ref.shape
    experts = slot_ref.shape[1]
    tile = nc.shape[2]

    @pl.when(step == 0)
    def _():
        h = hid_ref[...].astype(f32)
        scale = lax.rsqrt(jnp.mean(h * h, axis=1, keepdims=True) + norm_eps)
        normed = (h * scale * gain_ref[...]).astype(bf16)
        normed_ref[...] = normed
        for j in range(width // tile):
            nc[j] = normed[:, j * tile : (j + 1) * tile]
            nc[width // tile + j] = cot_ref[:, j * tile : (j + 1) * tile]
        ids = ids_ref[...]
        expert = iota((experts, tokens), 0)
        member = jnp.zeros((experts, tokens), f32)
        for k in range(ids.shape[0]):
            member += jnp.where(ids[k : k + 1, :] == expert, 1.0, 0.0)
        earlier = jnp.where(iota((tokens, tokens), 0) < iota((tokens, tokens), 1), 1.0, 0.0)
        position = mm(member.astype(bf16), earlier.astype(bf16))
        slot_t = jnp.where(member > 0.0, position, 99.0)
        slot_ref[...] = slot_t.T
        slot_t_ref[...] = slot_t
        which = iota((experts, HI, tokens), 1).astype(f32)
        chosen = jnp.where(slot_t[:, None, :] == which, 1.0, 0.0)
        p8[...] = chosen.reshape(experts * HI, tokens).astype(bf16)

    s1_ref[...] = mm(p8[...], nc[step]).astype(bf16)


def front(hidden, cotangent, gain, ids, experts):
    tokens, width = hidden.shape
    tile = min(512, width)
    steps = 2 * width // tile
    return pl.pallas_call(
        front_kernel,
        grid=(steps,),
        in_specs=[whole((tokens, width)), whole((tokens, width)), whole((1, width)), whole(ids.shape)],
        out_specs=[
            pl.BlockSpec((experts * HI, tile), lambda i: (0, i)),
            whole((tokens, width)),
            whole((tokens, experts)),
            whole((experts, tokens)),
        ],
        out_shape=[
            jax.ShapeDtypeStruct((experts * HI, 2 * width), bf16),
            jax.ShapeDtypeStruct((tokens, width), bf16),
            jax.ShapeDtypeStruct((tokens, experts), f32),
            jax.ShapeDtypeStruct((experts, tokens), f32),
        ],
        scratch_shapes=[pltpu.VMEM((steps, tokens, tile), bf16), pltpu.VMEM((experts * HI, tokens), bf16)],
        compiler_params=params(),
        cost_estimate=pl.CostEstimate(flops=4 * experts * HI * tokens * width, bytes_accessed=10_000_000, transcendentals=tokens),
    )(hidden, cotangent, gain, ids)


def second_kernel(normed_ref, cot_ref, slot_ref, slot_t_ref, router_ref, gates_ref, s2_ref):
    tokens, width = normed_ref.shape
    experts = slot_ref.shape[1]
    half = width // 2
    logits = mm(normed_ref[...], router_ref[...])
    weights = jnp.where(slot_ref[...] < 50.0, jnp.exp(logits), 0.0)
    gates = weights / jnp.sum(weights, axis=1, keepdims=True)
    gates_ref[...] = gates
    slot_t = slot_t_ref[...]
    gates_t = gates.T
    lane = iota((experts, MSG), 1)
    message = jnp.where(lane == 10, jnp.sum(jnp.where(slot_t < 50.0, 1.0, 0.0), axis=1, keepdims=True), 0.0)
    for s in range(10):
        message = message + jnp.where(
            lane == s, jnp.sum(jnp.where(slot_t == s, gates_t, 0.0), axis=1, keepdims=True), 0.0
        )
    sub = iota((experts, SUB, MSG), 1)
    spread = jnp.where(sub == 0, message[:, None, :], 0.0).reshape(experts * SUB, MSG)
    s2_ref[:, half:] = spread.astype(bf16)
    row = iota((experts, SUB, tokens), 1)
    chosen = jnp.where(slot_t[:, None, :] == (HI + row // 4).astype(f32), 1.0, 0.0)
    total = None
    for j in range(4):
        pick = jnp.where(row % 4 == j, chosen, 0.0).reshape(experts * SUB, tokens).astype(bf16)
        source = normed_ref if j < 2 else cot_ref
        term = mm(pick, source[:, (j % 2) * half : (j % 2 + 1) * half])
        total = term if total is None else total + term
    s2_ref[:, :half] = total.astype(bf16)


def second(normed, cotangent, slot, slot_t, router):
    tokens, width = normed.shape
    experts = slot.shape[1]
    return pl.pallas_call(
        second_kernel,
        out_shape=[
            jax.ShapeDtypeStruct((tokens, experts), f32),
            jax.ShapeDtypeStruct((experts * SUB, width // 2 + MSG), bf16),
        ],
        compiler_params=params(),
        cost_estimate=pl.CostEstimate(flops=4 * experts * SUB * tokens * width, bytes_accessed=4_000_000, transcendentals=tokens * experts),
    )(normed, cotangent, slot, slot_t, router)


def expert_rows(x, c, wg_ref, wu_ref, wd_ref):
    a = mm(x, wg_ref[...])
    b = mm(x, wu_ref[...])
    u = mm_nt(c, wd_ref[...])
    s = jax.nn.sigmoid(a)
    act = (a * s * b).astype(bf16)
    q = jnp.sum(act.astype(f32) * u, axis=1, keepdims=True)
    da = (u * b * s * (1.0 + a * (1.0 - s))).astype(bf16)
    db = (u * a * s).astype(bf16)
    return act, q, da, db


def rows_kernel(x_ref, c_ref, wg_ref, wu_ref, wd_ref, act_ref, da_ref, db_ref, q_ref, dx_ref):
    act, q, da, db = expert_rows(x_ref[...], c_ref[...], wg_ref, wu_ref, wd_ref)
    act_ref[...] = act
    da_ref[...] = da
    db_ref[...] = db
    sources = q_ref.shape[0]
    lane, which = iota((sources, HI, MSG), 2), iota((sources, HI, MSG), 1)
    q_ref[...] = jnp.sum(jnp.where(lane == which, q.reshape(sources, HI, 1), 0.0), axis=1)
    dx_ref[...] = (mm_nt(da, wg_ref[...]) + mm_nt(db, wu_ref[...])).astype(bf16)


def rows(r1, wg, wu, wd, extra):
    total, both = r1.shape
    width, hid = wg.shape
    block = min(256, total)
    one = pl.BlockSpec((block, hid), lambda i: (i, 0))
    return pl.pallas_call(
        rows_kernel,
        grid=(total // block,),
        in_specs=[
            pl.BlockSpec((block, width), lambda i: (i, 0)),
            pl.BlockSpec((block, width), lambda i: (i, 1)),
            whole(wg.shape, pipeline_mode=pl.Buffered(1)),
            whole(wu.shape, pipeline_mode=pl.Buffered(1)),
            whole(wd.shape, pipeline_mode=pl.Buffered(1)),
        ],
        out_specs=[one, one, one, pl.BlockSpec((block // HI, MSG), lambda i: (i, 0)), pl.BlockSpec((block, width), lambda i: (i, 0))],
        out_shape=[jax.ShapeDtypeStruct((total, hid), bf16)] * 3
        + [
            jax.ShapeDtypeStruct((total // HI, MSG), f32),
            jax.ShapeDtypeStruct((total, width + extra), bf16),
        ],
        compiler_params=params(),
        cost_estimate=pl.CostEstimate(flops=10 * total * width * hid, bytes_accessed=30_000_000, transcendentals=total * hid),
    )(r1, r1, wg, wu, wd)


def tail_kernel(limit, r2_ref, q8_ref, wg_ref, wu_ref, wd_ref, xc_ref, act_ref, da_ref, db_ref, msg_ref, scale_ref, q_sum):
    step, last = pl.program_id(0), pl.num_programs(0) - 1
    sources = q8_ref.shape[0]
    width = wg_ref.shape[0]
    half = width // 2
    total = 2 * sources

    @pl.when(step == 0)
    def _():
        chunk = min(32, sources)
        out_rows, in_rows = 2 * chunk, SUB * chunk
        index, column = iota((4 * out_rows, in_rows), 0), iota((4 * out_rows, in_rows), 1)
        pick = jnp.where(column == 4 * (index % out_rows) + index // out_rows, 1.0, 0.0).astype(bf16)
        for j in range(sources // chunk):
            part = mm(pick, r2_ref[j * in_rows : (j + 1) * in_rows, :half]).astype(bf16)
            for quarter in range(4):
                xc_ref[j * out_rows : (j + 1) * out_rows, quarter * half : (quarter + 1) * half] = part[
                    quarter * out_rows : (quarter + 1) * out_rows
                ]
        q_sum[...] = jnp.zeros_like(q_sum)

    act, q, da, db = expert_rows(xc_ref[:, :width], xc_ref[:, width:], wg_ref, wu_ref, wd_ref)
    act_ref[...] = act
    da_ref[...] = da
    db_ref[...] = db
    q_sum[...] += jnp.broadcast_to(q, q_sum.shape)

    @pl.when(step == last)
    def _():
        parity = iota((total, MSG), 0) % 2
        spread = jnp.where(iota((total, MSG), 1) == HI + parity, q_sum[...], 0.0).astype(bf16)
        gather = jnp.where(iota((sources, total), 1) // 2 == iota((sources, total), 0), 1.0, 0.0).astype(bf16)
        q_all = q8_ref[...].astype(bf16).astype(f32) + mm(gather, spread)
        meta = jnp.sum(r2_ref[:, half:].astype(f32).reshape(sources, SUB, MSG), axis=1)
        lane = iota((sources, MSG), 1)
        count = jnp.sum(jnp.where(lane == 10, meta, 0.0), axis=1, keepdims=True)
        lower = jnp.where(iota((sources, sources), 1) < iota((sources, sources), 0), 1.0, 0.0).astype(bf16)
        offset = mm(lower, jnp.broadcast_to(count, (sources, MSG)).astype(bf16))
        slot = jnp.where(lane < 10, lane, lane - 10).astype(f32)
        kept = (slot < count) & (offset + slot < limit) & (lane < 20)
        msg_ref[...] = jnp.where(kept, jnp.where(lane < 10, q_all, 1.0), 0.0)
        scale_ref[...] = jnp.where(kept & (lane < 10), meta, 0.0).astype(bf16)


def tail(r2, q8, wg, wu, wd, limit):
    sources = q8.shape[0]
    width, hid = wg.shape
    tile = min(256, hid)
    total = 2 * sources
    return pl.pallas_call(
        functools.partial(tail_kernel, float(limit)),
        grid=(hid // tile,),
        in_specs=[
            whole(r2.shape, pipeline_mode=pl.Buffered(1)),
            whole(q8.shape),
            pl.BlockSpec((width, tile), lambda i: (0, i)),
            pl.BlockSpec((width, tile), lambda i: (0, i)),
            pl.BlockSpec((tile, width), lambda i: (i, 0)),
        ],
        out_specs=[whole((total, 2 * width))]
        + [pl.BlockSpec((total, tile), lambda i: (0, i))] * 3
        + [whole((sources, MSG)), whole((sources, MSG))],
        out_shape=[jax.ShapeDtypeStruct((total, 2 * width), bf16)]
        + [jax.ShapeDtypeStruct((total, hid), bf16)] * 3
        + [jax.ShapeDtypeStruct((sources, MSG), f32), jax.ShapeDtypeStruct((sources, MSG), bf16)],
        scratch_shapes=[pltpu.VMEM((total, MSG), f32)],
        compiler_params=params(),
        cost_estimate=pl.CostEstimate(flops=12 * sources * width * hid, bytes_accessed=16_000_000, transcendentals=2 * sources * hid),
    )(r2, q8, wg, wu, wd)


def column_of(table):
    sources = table.shape[0]
    lane, which = iota((sources, HI, MSG), 2), iota((sources, HI, MSG), 1)
    spread = jnp.where(lane == which, table[:, None, :], 0.0)
    return jnp.sum(spread.reshape(sources * HI, MSG), axis=1, keepdims=True)


def tail_column_of(table):
    sources = table.shape[0]
    total = 2 * sources
    scatter = jnp.where(iota((total, sources), 0) // 2 == iota((total, sources), 1), 1.0, 0.0).astype(bf16)
    lane = HI + iota((total, MSG), 0) % 2
    return jnp.sum(jnp.where(iota((total, MSG), 1) == lane, mm(scatter, table), 0.0), axis=1, keepdims=True)


def tail_dx_kernel(da_ref, db_ref, wg_ref, wu_ref, x_ref, x2_ref, scale_ref, back_ref, out_ref, part_ref, s8, s2):
    step = pl.program_id(0)
    sources = scale_ref.shape[0]
    quarter = out_ref.shape[1]

    @pl.when(step == 0)
    def _():
        table = scale_ref[...]
        s8[...] = jnp.broadcast_to(column_of(table.astype(f32)), s8.shape)
        s2[...] = jnp.broadcast_to(tail_column_of(table), s2.shape)
        out_ref[...] = jnp.zeros_like(out_ref)

    dx2 = mm_nt(da_ref[...], wg_ref[...]) + mm_nt(db_ref[...], wu_ref[...])
    rounded = dx2.astype(bf16)
    chunk = min(32, sources)
    n_rows = SUB * chunk
    pick = jnp.where(iota((n_rows, 2 * chunk), 0) == 4 * iota((n_rows, 2 * chunk), 1) + step, 1.0, 0.0).astype(bf16)
    for j in range(sources // chunk):
        out_ref[j * n_rows : (j + 1) * n_rows, :] += mm(pick, rounded[j * 2 * chunk : (j + 1) * 2 * chunk]).astype(bf16)
    part = jnp.sum(x_ref[...].astype(f32) * back_ref[...].astype(f32) * s8[:, 0:1], axis=0, keepdims=True)
    part = part + jnp.sum(x2_ref[...].astype(f32) * dx2 * s2[:, 0:1], axis=0, keepdims=True)
    column = jnp.concatenate(
        [jnp.broadcast_to(part[:, j : j + MSG], (MSG, MSG)).T for j in range(0, quarter, MSG)], axis=0
    )
    dests = part_ref.shape[0] // SUB
    groups = quarter // dests // SUB
    column = column.reshape(dests, groups, SUB, MSG)
    lane = iota((dests, SUB, MSG), 2)
    spread = jnp.zeros((dests, SUB, MSG), f32)
    for g in range(groups):
        spread = jnp.where(lane == g, column[:, g], spread)
    part_ref[...] = spread.reshape(dests * SUB, MSG).astype(bf16)


def tail_dx(da, db, wg, wu, r1, xc2, scale, back):
    sources = scale.shape[0]
    width, hid = wg.shape
    quarter = width // 4
    main, total = sources * HI, 2 * sources
    columns = pl.BlockSpec((main, quarter), lambda i: (0, i))
    return pl.pallas_call(
        tail_dx_kernel,
        grid=(4,),
        in_specs=[
            whole(da.shape),
            whole(db.shape),
            pl.BlockSpec((quarter, hid), lambda i: (i, 0)),
            pl.BlockSpec((quarter, hid), lambda i: (i, 0)),
            columns,
            pl.BlockSpec((total, quarter), lambda i: (0, i)),
            whole(scale.shape),
            columns,
        ],
        out_specs=[
            pl.BlockSpec((sources * SUB, quarter), lambda i: (0, 4)),
            pl.BlockSpec((sources * SUB // 4, MSG), lambda i: (i, 0)),
        ],
        out_shape=[jax.ShapeDtypeStruct(back.shape, bf16), jax.ShapeDtypeStruct((sources * SUB, MSG), bf16)],
        scratch_shapes=[pltpu.VMEM((main, MSG), f32), pltpu.VMEM((total, MSG), f32)],
        input_output_aliases={7: 0},
        compiler_params=params(),
        cost_estimate=pl.CostEstimate(flops=4 * total * wg.size, bytes_accessed=18_000_000, transcendentals=0),
    )(da, db, wg, wu, r1, xc2, scale, back)


def weights_kernel(x_ref, c_ref, x2_ref, c2_ref, act_ref, da_ref, db_ref, act2_ref, da2_ref, db2_ref, scale_ref, dwg_ref, dwu_ref, dwd_ref, act_s, da_s, db_s):
    main = act_ref.shape[0]

    @pl.when(pl.program_id(0) == 0)
    def _():
        table = scale_ref[...]
        column, tail_column = column_of(table.astype(f32)), tail_column_of(table)
        for source, source2, target in ((act_ref, act2_ref, act_s), (da_ref, da2_ref, da_s), (db_ref, db2_ref, db_s)):
            target[:main] = (source[...].astype(f32) * column).astype(bf16)
            target[main:] = (source2[...].astype(f32) * tail_column).astype(bf16)

    def both(first, second, scaled):
        return mm_tn(first, scaled[:main]) + mm_tn(second, scaled[main:])

    dwg_ref[...] = both(x_ref[...], x2_ref[...], da_s).astype(bf16)
    dwu_ref[...] = both(x_ref[...], x2_ref[...], db_s).astype(bf16)
    dwd_ref[...] = (mm_tn(act_s[:main], c_ref[...]) + mm_tn(act_s[main:], c2_ref[...])).astype(bf16)


def weight_grads(r1, xc2, acts, acts2, scale, width, hid):
    main, tail_rows = r1.shape[0], xc2.shape[0]
    tile = min(256, width)
    steps = width // tile
    return pl.pallas_call(
        weights_kernel,
        grid=(steps,),
        in_specs=[
            pl.BlockSpec((main, tile), lambda i: (0, i)),
            pl.BlockSpec((main, tile), lambda i: (0, i + steps)),
            pl.BlockSpec((tail_rows, tile), lambda i: (0, i)),
            pl.BlockSpec((tail_rows, tile), lambda i: (0, i + steps)),
        ]
        + [whole((main, hid))] * 3
        + [whole((tail_rows, hid))] * 3
        + [whole(scale.shape)],
        out_specs=[
            pl.BlockSpec((tile, hid), lambda i: (i, 0)),
            pl.BlockSpec((tile, hid), lambda i: (i, 0)),
            pl.BlockSpec((hid, tile), lambda i: (0, i)),
        ],
        out_shape=[
            jax.ShapeDtypeStruct((width, hid), bf16),
            jax.ShapeDtypeStruct((width, hid), bf16),
            jax.ShapeDtypeStruct((hid, width), bf16),
        ],
        scratch_shapes=[pltpu.VMEM((main + tail_rows, hid), bf16)] * 3,
        compiler_params=params(),
        cost_estimate=pl.CostEstimate(flops=6 * (main + tail_rows) * width * hid, bytes_accessed=36_000_000, transcendentals=0),
    )(r1, r1, xc2, xc2, *acts, *acts2, scale)


def home_kernel(q_ref, slot_ref, gates_ref, normed_ref, part_ref, _, back_ref, dl_ref, gk_t_ref, router_part):
    step, last = pl.program_id(0), pl.num_programs(0) - 1
    experts = q_ref.shape[0]

    @pl.when(step == 0)
    def _():
        q_t = q_ref[...].T
        slot, gates = slot_ref[...], gates_ref[...]
        dgate = jnp.zeros_like(gates)
        kept = jnp.zeros_like(gates)
        for s in range(10):
            here = slot == s
            dgate = dgate + jnp.where(here, q_t[s : s + 1, :], 0.0)
            kept = kept + jnp.where(here, q_t[10 + s : 11 + s, :], 0.0)
        dsel = gates * (dgate - jnp.sum(gates * dgate, axis=1, keepdims=True))
        dl = dsel.astype(bf16)
        dl_ref[...] = dl
        gk_t_ref[...] = (gates.astype(bf16).astype(f32) * kept).T
        if experts < MSG:
            dl = jnp.concatenate([dl, jnp.zeros((dl.shape[0], MSG - experts), bf16)], axis=1)
        groups = router_part.shape[0]
        partial = mm_tn(normed_ref[...], dl).reshape(experts, groups, SUB, MSG)
        for g in range(groups):
            router_part[g] = partial[:, g].reshape(experts * SUB, MSG).astype(bf16)

    @pl.when(step < last)
    def _():
        back_ref[...] = router_part[jnp.minimum(step, router_part.shape[0] - 1)]

    @pl.when(step == last)
    def _():
        back_ref[...] = part_ref[...]


def home(q, slot, gates, normed, part, back):
    tokens, experts = slot.shape
    width = normed.shape[1]
    groups = width // experts // SUB
    first = (width + width // 4) // MSG
    return pl.pallas_call(
        home_kernel,
        grid=(groups + 1,),
        in_specs=[whole(q.shape), whole(slot.shape), whole(gates.shape), whole(normed.shape), whole(part.shape), pl.BlockSpec(memory_space=pl.ANY)],
        out_specs=[pl.BlockSpec((experts * SUB, MSG), lambda i: (0, first + i)), whole((tokens, experts)), whole((experts, tokens))],
        out_shape=[
            jax.ShapeDtypeStruct(back.shape, bf16),
            jax.ShapeDtypeStruct((tokens, experts), bf16),
            jax.ShapeDtypeStruct((experts, tokens), f32),
        ],
        scratch_shapes=[pltpu.VMEM((groups, experts * SUB, MSG), bf16)],
        input_output_aliases={5: 0},
        compiler_params=params(),
        cost_estimate=pl.CostEstimate(flops=2 * tokens * MSG * width, bytes_accessed=2_500_000, transcendentals=0),
    )(q, slot, gates, normed, part, back)


def sums_kernel(*refs):
    *parts, gain_ref, router_ref, gain_rows_ref, target_ref, out_ref = refs
    copies, n_rows, _ = out_ref.shape
    target = target_ref[...]
    row = iota(target.shape, 0)
    gain_parts = jnp.sum(gain_ref[...].astype(f32).reshape(copies, SUB, MSG), axis=0)
    pieces = []
    placed = jnp.zeros(target.shape, f32)
    for g, ref in enumerate(parts):
        piece = jnp.sum(ref[...].astype(f32).reshape(copies, SUB, MSG), axis=0)
        pieces.append(piece)
        own = slice(g * SUB, (g + 1) * SUB)
        value = gain_parts[:, g : g + 1] + jnp.sum(router_ref[own] * piece, axis=1, keepdims=True)
        placed = jnp.where(target == g * SUB + row, value / gain_rows_ref[own], placed)
    message = jnp.concatenate(pieces + [placed], axis=0)
    out_ref[...] = jnp.broadcast_to(message[None], out_ref.shape).astype(bf16)


def sums(rd, router_rows, gain_rows, target, experts, width):
    groups = width // experts // SUB
    first = (width + width // 4) // MSG
    block = (experts * SUB, MSG)
    specs = [pl.BlockSpec(block, functools.partial(lambda g, i: (0, first + g), g)) for g in range(groups + 1)]
    return pl.pallas_call(
        sums_kernel,
        grid=(1,),
        in_specs=specs + [whole(router_rows.shape), whole(gain_rows.shape), whole(target.shape)],
        out_specs=whole((experts, (groups + 1) * SUB, MSG)),
        out_shape=jax.ShapeDtypeStruct((experts, (groups + 1) * SUB, MSG), bf16),
        compiler_params=params(),
        cost_estimate=pl.CostEstimate(flops=experts * SUB * MSG * 8, bytes_accessed=2_000_000, transcendentals=0),
    )(*[rd] * (groups + 1), router_rows, gain_rows, target)


def final_kernel(dx_ref, ext_ref, slot_t_ref, gk_t_ref, dl_ref, router_ref, gain_ref, hid_ref, cot_ref, dh_ref, total):
    step, last = pl.program_id(0), pl.num_programs(0) - 1
    chunk, tokens = slot_t_ref.shape
    n_rows = chunk * SUB
    quarter = ext_ref.shape[1]
    slot, gk = slot_t_ref[...][:, None, :], gk_t_ref[...][:, None, :]
    which = iota((chunk, SUB, tokens), 1)

    def weights(mask):
        return jnp.where(mask, gk, 0.0).reshape(n_rows, tokens).astype(bf16)

    @pl.when(step == 0)
    def _():
        total[...] = mm_nt(dl_ref[...], router_ref[...])

    total[...] += mm_tn(weights(slot == which.astype(f32)), dx_ref[...])
    in_tail = slot == (HI + which // 4).astype(f32)
    for j in range(4):
        total[:, j * quarter : (j + 1) * quarter] += mm_tn(weights(in_tail & (which % 4 == j)), ext_ref[...])

    @pl.when(step == last)
    def _():
        h = hid_ref[...].astype(f32)
        scale = lax.rsqrt(jnp.mean(h * h, axis=1, keepdims=True) + norm_eps)
        gained = gain_ref[...] * total[...]
        mean = jnp.mean(gained * h, axis=1, keepdims=True)
        dh_ref[...] = (cot_ref[...].astype(f32) + scale * gained - h * (scale * scale * scale) * mean).astype(bf16)


def final(rd, slot_t, gk_t, dl, router, gain, hidden, cotangent):
    experts, tokens = slot_t.shape
    width = hidden.shape[1]
    chunk = min(32, experts)
    steps = experts // chunk
    return pl.pallas_call(
        final_kernel,
        grid=(steps,),
        in_specs=[
            pl.BlockSpec((chunk * SUB, width), lambda i: (i, 0)),
            pl.BlockSpec((chunk * SUB, width // 4), lambda i: (i, 4)),
            pl.BlockSpec((chunk, tokens), lambda i: (i, 0)),
            pl.BlockSpec((chunk, tokens), lambda i: (i, 0)),
            whole(dl.shape),
            whole(router.shape),
            whole((1, width)),
            whole((tokens, width)),
            whole((tokens, width)),
        ],
        out_specs=whole((tokens, width)),
        out_shape=jax.ShapeDtypeStruct((tokens, width), bf16),
        scratch_shapes=[pltpu.VMEM((tokens, width), f32)],
        compiler_params=params(),
        cost_estimate=pl.CostEstimate(flops=4 * experts * SUB * tokens * width, bytes_accessed=9_000_000, transcendentals=tokens),
    )(rd, rd, slot_t, gk_t, dl, router, gain, hidden, cotangent)


def place_kernel(sums_ref, router_ref, gain_ref):
    experts, n_rows, _ = sums_ref.shape
    rows_each = n_rows - SUB
    received = sums_ref[...].astype(f32)
    router_ref[...] = received[:, :rows_each].reshape(experts * rows_each, MSG)[:, : router_ref.shape[1]]
    gain_ref[...] = jnp.sum(received[:, rows_each:].reshape(gain_ref.shape[0], -1, MSG), axis=1)


def place(received, width, experts):
    return pl.pallas_call(
        place_kernel,
        out_shape=[jax.ShapeDtypeStruct((width, experts), f32), jax.ShapeDtypeStruct((width // MSG, MSG), f32)],
        compiler_params=params(),
        cost_estimate=pl.CostEstimate(flops=received.size, bytes_accessed=2_000_000, transcendentals=0),
    )(received)


def on_device(hidden, cotangent, norm_gain, router, w_gate, w_up, w_down, expert_ids):
    tokens, width = hidden.shape
    top = expert_ids.shape[1]
    experts = router.shape[1]
    half, quarter = width // 2, width // 4
    limit = tokens * top
    gain = norm_gain.reshape(1, width)
    wg, wu, wd = w_gate[0], w_up[0], w_down[0]
    own = width // experts
    extra = quarter + (own // SUB + 1) * MSG

    me = lax.axis_index(AXES)
    router_rows = lax.dynamic_slice_in_dim(router, me * own, own, 0).astype(f32)
    router_rows = jnp.pad(router_rows, ((0, 0), (0, MSG - experts)))
    gain_rows = jnp.broadcast_to(lax.dynamic_slice_in_dim(norm_gain, me * own, own, 0)[:, None], (own, MSG))
    target = lax.broadcasted_iota(jnp.int32, (SUB, MSG), 1) - (me % (MSG // own)) * own

    s1, normed, slot, slot_t = front(hidden, cotangent, gain, expert_ids.T, experts)
    r1 = exchange(s1.reshape(experts, HI, 2 * width)).reshape(experts * HI, 2 * width)
    gates, s2 = second(normed, cotangent, slot, slot_t, router)
    r2 = exchange(s2.reshape(experts, SUB, half + MSG)).reshape(experts * SUB, half + MSG)
    act, da, db, q8, back = rows(r1, wg, wu, wd, extra)
    xc2, act2, da2, db2, q_msg, scale = tail(r2, q8, wg, wu, wd, limit)
    q_home = exchange(q_msg.reshape(experts, 1, MSG)).reshape(experts, MSG)
    back, part = tail_dx(da2, db2, wg, wu, r1, xc2, scale, back)
    back, dl, gk_t = home(q_home, slot, gates, normed, part, back)
    scale, dl = lax.optimization_barrier((scale, dl))
    d_wgate, d_wup, d_wdown = weight_grads(r1, xc2, (act, da, db), (act2, da2, db2), scale, width, wg.shape[1])
    rd = exchange(back.reshape(experts, HI, width + extra)).reshape(experts * HI, width + extra)
    d_wgate, gain_rows = lax.optimization_barrier((d_wgate, gain_rows))
    message = sums(rd, router_rows, gain_rows, target, experts, width)
    received = exchange(message)
    d_hidden = final(rd, slot_t, gk_t, dl, router, gain, hidden, cotangent)
    d_router, d_gain = place(received, width, experts)
    return (d_hidden, d_gain.reshape(width), d_router, d_wgate[None], d_wup[None], d_wdown[None])


def solution(mesh):
    rows_spec, stack_spec = P(AXES, None), P(AXES, None, None)
    in_specs = (rows_spec, rows_spec, P(), P(), stack_spec, stack_spec, stack_spec, rows_spec)
    out_specs = (rows_spec, P(), P(), stack_spec, stack_spec, stack_spec)
    return jax.shard_map(on_device, mesh=mesh, in_specs=in_specs, out_specs=out_specs, check_vma=False)
```

```python
import functools

import jax
import jax.numpy as jnp
from jax import lax
from jax.experimental import pallas as pl
from jax.experimental.pallas import tpu as pltpu
from jax.sharding import PartitionSpec as P

norm_eps = 1e-06
HI = 8
SUB = 8
MSG = 128
TILE = 256
AXES = ("seq", "exp")
bf16, f32 = jnp.bfloat16, jnp.float32


def params(mib=60):
    return pltpu.CompilerParams(vmem_limit_bytes=mib * 1024 * 1024)


def whole(shape, **kw):
    return pl.BlockSpec(shape, lambda *_: (0,) * len(shape), **kw)


def iota(shape, dim):
    return lax.broadcasted_iota(jnp.int32, shape, dim)


def mm(a, b):
    return jnp.dot(a, b, preferred_element_type=f32)


def mm_nt(a, b):
    return lax.dot_general(a, b, (((1,), (1,)), ((), ())), preferred_element_type=f32)


def mm_tn(a, b):
    return lax.dot_general(a, b, (((0,), (0,)), ((), ())), preferred_element_type=f32)


def exchange(x):
    return lax.all_to_all(x, AXES, split_axis=0, concat_axis=0, tiled=True)


def slots_chosen(slot_t):
    experts, tokens = slot_t.shape
    which = iota((experts, HI, tokens), 1).astype(f32)
    chosen = jnp.where(slot_t[:, None, :] == which, 1.0, 0.0)
    return chosen.reshape(experts * HI, tokens).astype(bf16)


def quarter_chosen(slot_t, j):
    experts, tokens = slot_t.shape
    row = iota((experts, SUB, tokens), 1)
    chosen = (slot_t[:, None, :] == (HI + row // 4).astype(f32)) & (row % 4 == j)
    return jnp.where(chosen, 1.0, 0.0).reshape(experts * SUB, tokens).astype(bf16)


def front_kernel(hid_ref, gain_ref, ids_ref, out_ref, normed_ref, slot_ref, slot_t_ref, tiles, p8):
    step = pl.program_id(0)
    tokens = hid_ref.shape[0]
    experts = slot_ref.shape[1]
    tile = tiles.shape[2]

    @pl.when(step == 0)
    def _():
        h = hid_ref[...].astype(f32)
        scale = lax.rsqrt(jnp.mean(h * h, axis=1, keepdims=True) + norm_eps)
        normed = (h * scale * gain_ref[...]).astype(bf16)
        normed_ref[...] = normed
        for j in range(4):
            tiles[j] = normed[:, j * tile : (j + 1) * tile]
        ids = ids_ref[...]
        expert = iota((experts, tokens), 0)
        member = jnp.zeros((experts, tokens), f32)
        for k in range(ids.shape[0]):
            member += jnp.where(ids[k : k + 1, :] == expert, 1.0, 0.0)
        earlier = jnp.where(iota((tokens, tokens), 0) < iota((tokens, tokens), 1), 1.0, 0.0)
        position = mm(member.astype(bf16), earlier.astype(bf16))
        slot_t = jnp.where(member > 0.0, position, 99.0)
        slot_ref[...] = slot_t.T
        slot_t_ref[...] = slot_t
        p8[...] = slots_chosen(slot_t)

    @pl.when(step < 4)
    def _():
        out_ref[...] = mm(p8[...], tiles[jnp.minimum(step, 3)]).astype(bf16)

    @pl.when(step == 4)
    def _():
        slot_t = slot_t_ref[...]
        total = mm(quarter_chosen(slot_t, 0), tiles[0])
        for j in range(1, 4):
            total = total + mm(quarter_chosen(slot_t, j), tiles[j])
        out_ref[...] = total.astype(bf16)


def front(hidden, gain, ids, experts):
    tokens, width = hidden.shape
    tile = width // 4
    return pl.pallas_call(
        front_kernel,
        grid=(5,),
        in_specs=[whole((tokens, width)), whole((1, width)), whole(ids.shape)],
        out_specs=[
            pl.BlockSpec((experts * HI, tile), lambda i: (0, i)),
            whole((tokens, width)),
            whole((tokens, experts)),
            whole((experts, tokens)),
        ],
        out_shape=[
            jax.ShapeDtypeStruct((experts * HI, width + tile), bf16),
            jax.ShapeDtypeStruct((tokens, width), bf16),
            jax.ShapeDtypeStruct((tokens, experts), f32),
            jax.ShapeDtypeStruct((experts, tokens), f32),
        ],
        scratch_shapes=[pltpu.VMEM((4, tokens, tile), bf16), pltpu.VMEM((experts * HI, tokens), bf16)],
        compiler_params=params(),
        cost_estimate=pl.CostEstimate(flops=4 * experts * HI * tokens * width, bytes_accessed=7_000_000, transcendentals=tokens),
    )(hidden, gain, ids)


def second_kernel(normed_ref, cot_ref, slot_ref, slot_t_ref, router_ref, gates_ref, out_ref, tiles, p8, p2, meta):
    step, last = pl.program_id(0), pl.num_programs(0) - 1
    experts = slot_ref.shape[1]
    count = tiles.shape[0]
    per = count // 4

    @pl.when(step == 0)
    def _():
        logits = mm(normed_ref[...], router_ref[...])
        weights = jnp.where(slot_ref[...] < 50.0, jnp.exp(logits), 0.0)
        gates = weights / jnp.sum(weights, axis=1, keepdims=True)
        gates_ref[...] = gates
        slot_t = slot_t_ref[...]
        gates_t = gates.T
        lane = iota((experts, MSG), 1)
        message = jnp.where(lane == 10, jnp.sum(jnp.where(slot_t < 50.0, 1.0, 0.0), axis=1, keepdims=True), 0.0)
        for s in range(10):
            message = message + jnp.where(
                lane == s, jnp.sum(jnp.where(slot_t == s, gates_t, 0.0), axis=1, keepdims=True), 0.0
            )
        sub = iota((experts, SUB, MSG), 1)
        meta[...] = jnp.where(sub == 0, message[:, None, :], 0.0).reshape(experts * SUB, MSG).astype(bf16)
        for j in range(count):
            tiles[j] = cot_ref[:, j * MSG : (j + 1) * MSG]
        p8[...] = slots_chosen(slot_t)
        for j in range(4):
            p2[j] = quarter_chosen(slot_t, j)

    @pl.when(step < count)
    def _():
        out_ref[...] = mm(p8[...], tiles[jnp.minimum(step, count - 1)]).astype(bf16)

    @pl.when((step >= count) & (step < last))
    def _():
        at = jnp.clip(step - count, 0, per - 1)
        total = mm(p2[0], tiles[at])
        for j in range(1, 4):
            total = total + mm(p2[j], tiles[j * per + at])
        out_ref[...] = total.astype(bf16)

    @pl.when(step == last)
    def _():
        out_ref[...] = meta[...]


def second(normed, cotangent, slot, slot_t, router):
    tokens, width = normed.shape
    experts = slot.shape[1]
    count = width // MSG
    steps = count + count // 4 + 1
    n_rows = experts * HI
    return pl.pallas_call(
        second_kernel,
        grid=(steps,),
        in_specs=[whole(normed.shape), whole(cotangent.shape), whole(slot.shape), whole(slot_t.shape), whole(router.shape)],
        out_specs=[whole((tokens, experts)), pl.BlockSpec((n_rows, MSG), lambda i: (0, i))],
        out_shape=[
            jax.ShapeDtypeStruct((tokens, experts), f32),
            jax.ShapeDtypeStruct((n_rows, steps * MSG), bf16),
        ],
        scratch_shapes=[
            pltpu.VMEM((count, tokens, MSG), bf16),
            pltpu.VMEM((n_rows, tokens), bf16),
            pltpu.VMEM((4, n_rows, tokens), bf16),
            pltpu.VMEM((n_rows, MSG), bf16),
        ],
        compiler_params=params(),
        cost_estimate=pl.CostEstimate(flops=4 * n_rows * tokens * width, bytes_accessed=8_000_000, transcendentals=tokens * experts),
    )(normed, cotangent, slot, slot_t, router)


def turn_kernel(wg_ref, wu_ref, wd_ref, both_ref, wd_t_ref):
    both_ref[: wg_ref.shape[1]] = wg_ref[...].T
    both_ref[wg_ref.shape[1] :] = wu_ref[...].T
    wd_t_ref[...] = wd_ref[...].T


def turn(wg, wu, wd):
    width, hid = wg.shape
    tile = min(TILE, hid)
    tall, wide = pl.BlockSpec((width, tile), lambda i: (0, i)), pl.BlockSpec((tile, width), lambda i: (i, 0))
    return pl.pallas_call(
        turn_kernel,
        grid=(hid // tile,),
        in_specs=[tall, tall, wide],
        out_specs=[pl.BlockSpec((2 * tile, width), lambda i: (i, 0)), tall],
        out_shape=[jax.ShapeDtypeStruct((2 * hid, width), bf16), jax.ShapeDtypeStruct((width, hid), bf16)],
        compiler_params=params(),
        cost_estimate=pl.CostEstimate(flops=3 * wg.size, bytes_accessed=19_000_000, transcendentals=0),
    )(wg, wu, wd)


def gather_quarters(ext_ref, target):
    n_rows, quarter = ext_ref.shape
    sources = n_rows // SUB
    chunk = min(32, sources)
    out_rows, in_rows = 2 * chunk, SUB * chunk
    index, column = iota((4 * out_rows, in_rows), 0), iota((4 * out_rows, in_rows), 1)
    pick = jnp.where(column == 4 * (index % out_rows) + index // out_rows, 1.0, 0.0).astype(bf16)
    for j in range(sources // chunk):
        part = mm(pick, ext_ref[j * in_rows : (j + 1) * in_rows, :]).astype(bf16)
        for q in range(4):
            target[j * out_rows : (j + 1) * out_rows, q * quarter : (q + 1) * quarter] = part[q * out_rows : (q + 1) * out_rows]


def x_kernel(x_ref, ext_ref, wg_ref, wu_ref, act_ref, fa_ref, fb_ref, x2_ref, held):
    step = pl.program_id(0)

    @pl.when(step < 4)
    def _():
        held[...] = x_ref[...]

    @pl.when(step == 4)
    def _():
        gather_quarters(ext_ref, held)
        x2_ref[...] = held[...]

    a = mm(held[...], wg_ref[...])
    b = mm(held[...], wu_ref[...])
    s = jax.nn.sigmoid(a)
    act_ref[...] = (a * s * b).astype(bf16)
    fa_ref[...] = (b * s * (1.0 + a * (1.0 - s))).astype(bf16)
    fb_ref[...] = (a * s).astype(bf16)


def x_side(r1, wg, wu):
    width, hid = wg.shape
    main = r1.shape[0]
    block = main // 4
    total = 5 * block
    out = pl.BlockSpec((block, hid), lambda i: (i, 0))
    return pl.pallas_call(
        x_kernel,
        grid=(5,),
        in_specs=[
            pl.BlockSpec((block, width), lambda i: (jnp.minimum(i, 3), 0)),
            pl.BlockSpec((main, width // 4), lambda i: (0, 4)),
            whole(wg.shape),
            whole(wu.shape),
        ],
        out_specs=[out, out, out, whole((block, width))],
        out_shape=[
            jax.ShapeDtypeStruct((total, hid), bf16),
            jax.ShapeDtypeStruct((total, hid), bf16),
            jax.ShapeDtypeStruct((total, hid), bf16),
            jax.ShapeDtypeStruct((block, width), bf16),
        ],
        scratch_shapes=[pltpu.VMEM((block, width), bf16)],
        compiler_params=params(),
        cost_estimate=pl.CostEstimate(flops=4 * total * wg.size, bytes_accessed=24_000_000, transcendentals=total * hid),
    )(r1, r1, wg, wu)


def folded(product):
    total = product[:, :MSG]
    for j in range(1, product.shape[1] // MSG):
        total = total + product[:, j * MSG : (j + 1) * MSG]
    return total


def c_kernel(limit, c_ref, ext_ref, meta_ref, wd_t_ref, act_ref, fa_ref, fb_ref, dab_ref, c2_ref, msg_ref, scale_ref, q8, q2):
    step, last = pl.program_id(0), pl.num_programs(0) - 1
    sources = msg_ref.shape[0]
    main, tail = c_ref.shape[0], c2_ref.shape[0]
    tile = act_ref.shape[1]

    @pl.when(step == 0)
    def _():
        gather_quarters(ext_ref, c2_ref)
        q8[...] = jnp.zeros_like(q8)
        q2[...] = jnp.zeros_like(q2)

    for rows, c, total in ((slice(0, main), c_ref, q8), (slice(main, main + tail), c2_ref, q2)):
        u = mm(c[...], wd_t_ref[...])
        total[...] += folded(act_ref[rows].astype(f32) * u)
        dab_ref[rows, :tile] = (u * fa_ref[rows].astype(f32)).astype(bf16)
        dab_ref[rows, tile:] = (u * fb_ref[rows].astype(f32)).astype(bf16)

    @pl.when(step == last)
    def _():
        lane, which = iota((sources, HI, MSG), 2), iota((sources, HI, MSG), 1)
        q = jnp.sum(q8[...], axis=1, keepdims=True)
        q_rows = jnp.sum(jnp.where(lane == which, q.reshape(sources, HI, 1), 0.0), axis=1).astype(bf16).astype(f32)
        q = jnp.sum(q2[...], axis=1, keepdims=True)
        parity = iota((tail, MSG), 0) % 2
        spread = jnp.where(iota((tail, MSG), 1) == HI + parity, q, 0.0).astype(bf16)
        gather = jnp.where(iota((sources, tail), 1) // 2 == iota((sources, tail), 0), 1.0, 0.0).astype(bf16)
        q_rows = q_rows + mm(gather, spread)
        meta = jnp.sum(meta_ref[...].astype(f32).reshape(sources, SUB, MSG), axis=1)
        lane = iota((sources, MSG), 1)
        count = jnp.sum(jnp.where(lane == 10, meta, 0.0), axis=1, keepdims=True)
        lower = jnp.where(iota((sources, sources), 1) < iota((sources, sources), 0), 1.0, 0.0).astype(bf16)
        offset = mm(lower, jnp.broadcast_to(count, (sources, MSG)).astype(bf16))
        slot = jnp.where(lane < 10, lane, lane - 10).astype(f32)
        kept = (slot < count) & (offset + slot < limit) & (lane < 20)
        msg_ref[...] = jnp.where(kept, jnp.where(lane < 10, q_rows, 1.0), 0.0)
        scale_ref[...] = jnp.where(kept & (lane < 10), meta, 0.0).astype(bf16)


def c_side(r2, wd_t, act, fa, fb, limit):
    width, hid = wd_t.shape
    main = r2.shape[0]
    sources, tail = main // SUB, main // 4
    total = main + tail
    tile = min(TILE, hid)

    def columns(n_rows, n_columns):
        return pl.BlockSpec((n_rows, n_columns), lambda i: (0, i))

    return pl.pallas_call(
        functools.partial(c_kernel, float(limit)),
        grid=(hid // tile,),
        in_specs=[
            whole((main, width)),
            pl.BlockSpec((main, width // 4), lambda i: (0, 4)),
            pl.BlockSpec((main, MSG), lambda i: (0, (width + width // 4) // MSG)),
            columns(width, tile),
            columns(total, tile),
            columns(total, tile),
            columns(total, tile),
        ],
        out_specs=[columns(total, 2 * tile), whole((tail, width)), whole((sources, MSG)), whole((sources, MSG))],
        out_shape=[
            jax.ShapeDtypeStruct((total, 2 * hid), bf16),
            jax.ShapeDtypeStruct((tail, width), bf16),
            jax.ShapeDtypeStruct((sources, MSG), f32),
            jax.ShapeDtypeStruct((sources, MSG), bf16),
        ],
        scratch_shapes=[pltpu.VMEM((main, MSG), f32), pltpu.VMEM((tail, MSG), f32)],
        compiler_params=params(),
        cost_estimate=pl.CostEstimate(flops=2 * total * wd_t.size, bytes_accessed=20_000_000, transcendentals=0),
    )(r2, r2, r2, wd_t, act, fa, fb)


def column_of(table):
    sources = table.shape[0]
    lane, which = iota((sources, HI, MSG), 2), iota((sources, HI, MSG), 1)
    spread = jnp.where(lane == which, table[:, None, :], 0.0)
    return jnp.sum(spread.reshape(sources * HI, MSG), axis=1, keepdims=True)


def tail_column_of(table):
    sources = table.shape[0]
    total = 2 * sources
    scatter = jnp.where(iota((total, sources), 0) // 2 == iota((total, sources), 1), 1.0, 0.0).astype(bf16)
    lane = HI + iota((total, MSG), 0) % 2
    return jnp.sum(jnp.where(iota((total, MSG), 1) == lane, mm(scatter, table), 0.0), axis=1, keepdims=True)


def dx_kernel(dab_ref, both_ref, x_ref, x2_ref, scale_ref, out_ref, part_ref, ext, s8, s2):
    step = pl.program_id(0)
    sources = scale_ref.shape[0]
    main, quarter = out_ref.shape

    @pl.when(step == 0)
    def _():
        table = scale_ref[...]
        s8[...] = jnp.broadcast_to(column_of(table.astype(f32)), s8.shape)
        s2[...] = jnp.broadcast_to(tail_column_of(table), s2.shape)
        ext[...] = jnp.zeros_like(ext)

    @pl.when(step < 4)
    def _():
        dx = mm(dab_ref[...], both_ref[...])
        rounded = dx.astype(bf16)
        out_ref[...] = rounded[:main]
        chunk = min(32, sources)
        n_rows = SUB * chunk
        pick = jnp.where(iota((n_rows, 2 * chunk), 0) == 4 * iota((n_rows, 2 * chunk), 1) + step, 1.0, 0.0).astype(bf16)
        for j in range(sources // chunk):
            tail = rounded[main + j * 2 * chunk : main + (j + 1) * 2 * chunk]
            ext[j * n_rows : (j + 1) * n_rows, :] += mm(pick, tail).astype(bf16)
        part = jnp.sum(x_ref[...].astype(f32) * dx[:main] * s8[:, 0:1], axis=0, keepdims=True)
        part = part + jnp.sum(x2_ref[...].astype(f32) * dx[main:] * s2[:, 0:1], axis=0, keepdims=True)
        column = jnp.concatenate(
            [jnp.broadcast_to(part[:, j : j + MSG], (MSG, MSG)).T for j in range(0, quarter, MSG)], axis=0
        )
        dests = part_ref.shape[0] // SUB
        groups = quarter // dests // SUB
        column = column.reshape(dests, groups, SUB, MSG)
        lane = iota((dests, SUB, MSG), 2)
        spread = jnp.zeros((dests, SUB, MSG), f32)
        for g in range(groups):
            spread = jnp.where(lane == g, column[:, g], spread)
        part_ref[...] = spread.reshape(dests * SUB, MSG).astype(bf16)

    @pl.when(step == 4)
    def _():
        out_ref[...] = ext[...]


def dx_side(dab, both, r1, x2, scale, extra):
    sources = scale.shape[0]
    twice, width = both.shape
    quarter = width // 4
    main, total = sources * HI, 2 * sources

    def columns(n_rows):
        return pl.BlockSpec((n_rows, quarter), lambda i: (0, jnp.minimum(i, 3)))

    return pl.pallas_call(
        dx_kernel,
        grid=(5,),
        in_specs=[whole(dab.shape), columns(twice), columns(main), columns(total), whole(scale.shape)],
        out_specs=[
            pl.BlockSpec((main, quarter), lambda i: (0, i)),
            pl.BlockSpec((main // 4, MSG), lambda i: (jnp.minimum(i, 3), 0)),
        ],
        out_shape=[jax.ShapeDtypeStruct((main, width + extra), bf16), jax.ShapeDtypeStruct((main, MSG), bf16)],
        scratch_shapes=[pltpu.VMEM((main, quarter), bf16), pltpu.VMEM((main, MSG), f32), pltpu.VMEM((total, MSG), f32)],
        compiler_params=params(),
        cost_estimate=pl.CostEstimate(flops=2 * (main + total) * both.size, bytes_accessed=20_000_000, transcendentals=0),
    )(dab, both, r1, x2, scale)


def weights_kernel(x_ref, c_ref, x2_ref, c2_ref, act_ref, dab_ref, scale_ref, dwg_ref, dwu_ref, dwd_ref, act_s, dab_s):
    main = x_ref.shape[0]
    hid = act_ref.shape[1]
    tile = min(TILE, hid)

    @pl.when(pl.program_id(0) == 0)
    def _():
        table = scale_ref[...]
        column, tail_column = column_of(table.astype(f32)), tail_column_of(table)
        for source, target in ((act_ref, act_s), (dab_ref, dab_s)):
            target[:main] = (source[:main].astype(f32) * column).astype(bf16)
            target[main:] = (source[main:].astype(f32) * tail_column).astype(bf16)

    both = (mm_tn(x_ref[...], dab_s[:main]) + mm_tn(x2_ref[...], dab_s[main:])).astype(bf16)
    for j in range(hid // tile):
        dwg_ref[:, j * tile : (j + 1) * tile] = both[:, 2 * j * tile : (2 * j + 1) * tile]
        dwu_ref[:, j * tile : (j + 1) * tile] = both[:, (2 * j + 1) * tile : (2 * j + 2) * tile]
    dwd_ref[...] = (mm_tn(act_s[:main], c_ref[...]) + mm_tn(act_s[main:], c2_ref[...])).astype(bf16)


def weight_grads(r1, r2, x2, c2, act, dab, scale):
    total, hid = act.shape
    main, width = r1.shape[0], x2.shape[1]
    tile = min(256, width)
    steps = width // tile

    def columns(n_rows):
        return pl.BlockSpec((n_rows, tile), lambda i: (0, i))

    return pl.pallas_call(
        weights_kernel,
        grid=(steps,),
        in_specs=[columns(main), columns(main), columns(total - main), columns(total - main)]
        + [whole(act.shape), whole(dab.shape), whole(scale.shape)],
        out_specs=[pl.BlockSpec((tile, hid), lambda i: (i, 0)), pl.BlockSpec((tile, hid), lambda i: (i, 0)), columns(hid)],
        out_shape=[
            jax.ShapeDtypeStruct((width, hid), bf16),
            jax.ShapeDtypeStruct((width, hid), bf16),
            jax.ShapeDtypeStruct((hid, width), bf16),
        ],
        scratch_shapes=[pltpu.VMEM(act.shape, bf16), pltpu.VMEM(dab.shape, bf16)],
        compiler_params=params(),
        cost_estimate=pl.CostEstimate(flops=6 * total * width * hid, bytes_accessed=36_000_000, transcendentals=0),
    )(r1, r2, x2, c2, act, dab, scale)


def home_kernel(q_ref, slot_ref, gates_ref, normed_ref, part_ref, _, back_ref, dl_ref, gk_t_ref, router_part):
    step, last = pl.program_id(0), pl.num_programs(0) - 1
    experts = q_ref.shape[0]

    @pl.when(step == 0)
    def _():
        q_t = q_ref[...].T
        slot, gates = slot_ref[...], gates_ref[...]
        dgate = jnp.zeros_like(gates)
        kept = jnp.zeros_like(gates)
        for s in range(10):
            here = slot == s
            dgate = dgate + jnp.where(here, q_t[s : s + 1, :], 0.0)
            kept = kept + jnp.where(here, q_t[10 + s : 11 + s, :], 0.0)
        dsel = gates * (dgate - jnp.sum(gates * dgate, axis=1, keepdims=True))
        dl = dsel.astype(bf16)
        dl_ref[...] = dl
        gk_t_ref[...] = (gates.astype(bf16).astype(f32) * kept).T
        if experts < MSG:
            dl = jnp.concatenate([dl, jnp.zeros((dl.shape[0], MSG - experts), bf16)], axis=1)
        groups = router_part.shape[0]
        partial = mm_tn(normed_ref[...], dl).reshape(experts, groups, SUB, MSG)
        for g in range(groups):
            router_part[g] = partial[:, g].reshape(experts * SUB, MSG).astype(bf16)

    @pl.when(step < last)
    def _():
        back_ref[...] = router_part[jnp.minimum(step, router_part.shape[0] - 1)]

    @pl.when(step == last)
    def _():
        back_ref[...] = part_ref[...]


def home(q, slot, gates, normed, part, back):
    tokens, experts = slot.shape
    width = normed.shape[1]
    groups = width // experts // SUB
    first = (width + width // 4) // MSG
    return pl.pallas_call(
        home_kernel,
        grid=(groups + 1,),
        in_specs=[whole(q.shape), whole(slot.shape), whole(gates.shape), whole(normed.shape), whole(part.shape), pl.BlockSpec(memory_space=pl.ANY)],
        out_specs=[pl.BlockSpec((experts * SUB, MSG), lambda i: (0, first + i)), whole((tokens, experts)), whole((experts, tokens))],
        out_shape=[
            jax.ShapeDtypeStruct(back.shape, bf16),
            jax.ShapeDtypeStruct((tokens, experts), bf16),
            jax.ShapeDtypeStruct((experts, tokens), f32),
        ],
        scratch_shapes=[pltpu.VMEM((groups, experts * SUB, MSG), bf16)],
        input_output_aliases={5: 0},
        compiler_params=params(),
        cost_estimate=pl.CostEstimate(flops=2 * tokens * MSG * width, bytes_accessed=2_500_000, transcendentals=0),
    )(q, slot, gates, normed, part, back)


def sums_kernel(*refs):
    *parts, gain_ref, router_ref, gain_rows_ref, target_ref, out_ref = refs
    copies, n_rows, _ = out_ref.shape
    target = target_ref[...]
    row = iota(target.shape, 0)
    gain_parts = jnp.sum(gain_ref[...].astype(f32).reshape(copies, SUB, MSG), axis=0)
    pieces = []
    placed = jnp.zeros(target.shape, f32)
    for g, ref in enumerate(parts):
        piece = jnp.sum(ref[...].astype(f32).reshape(copies, SUB, MSG), axis=0)
        pieces.append(piece)
        own = slice(g * SUB, (g + 1) * SUB)
        value = gain_parts[:, g : g + 1] + jnp.sum(router_ref[own] * piece, axis=1, keepdims=True)
        placed = jnp.where(target == g * SUB + row, value / gain_rows_ref[own], placed)
    message = jnp.concatenate(pieces + [placed], axis=0)
    out_ref[...] = jnp.broadcast_to(message[None], out_ref.shape).astype(bf16)


def sums(rd, router_rows, gain_rows, target, experts, width):
    groups = width // experts // SUB
    first = (width + width // 4) // MSG
    block = (experts * SUB, MSG)
    specs = [pl.BlockSpec(block, functools.partial(lambda g, i: (0, first + g), g)) for g in range(groups + 1)]
    return pl.pallas_call(
        sums_kernel,
        grid=(1,),
        in_specs=specs + [whole(router_rows.shape), whole(gain_rows.shape), whole(target.shape)],
        out_specs=whole((experts, (groups + 1) * SUB, MSG)),
        out_shape=jax.ShapeDtypeStruct((experts, (groups + 1) * SUB, MSG), bf16),
        compiler_params=params(),
        cost_estimate=pl.CostEstimate(flops=experts * SUB * MSG * 8, bytes_accessed=2_000_000, transcendentals=0),
    )(*[rd] * (groups + 1), router_rows, gain_rows, target)


def final_kernel(dx_ref, ext_ref, slot_t_ref, gk_t_ref, dl_ref, router_ref, gain_ref, hid_ref, cot_ref, dh_ref, total):
    step, last = pl.program_id(0), pl.num_programs(0) - 1
    chunk, tokens = slot_t_ref.shape
    n_rows = chunk * SUB
    quarter = ext_ref.shape[1]
    slot, gk = slot_t_ref[...][:, None, :], gk_t_ref[...][:, None, :]
    which = iota((chunk, SUB, tokens), 1)

    def weights(mask):
        return jnp.where(mask, gk, 0.0).reshape(n_rows, tokens).astype(bf16)

    @pl.when(step == 0)
    def _():
        total[...] = mm_nt(dl_ref[...], router_ref[...])

    total[...] += mm_tn(weights(slot == which.astype(f32)), dx_ref[...])
    in_tail = slot == (HI + which // 4).astype(f32)
    for j in range(4):
        total[:, j * quarter : (j + 1) * quarter] += mm_tn(weights(in_tail & (which % 4 == j)), ext_ref[...])

    @pl.when(step == last)
    def _():
        h = hid_ref[...].astype(f32)
        scale = lax.rsqrt(jnp.mean(h * h, axis=1, keepdims=True) + norm_eps)
        gained = gain_ref[...] * total[...]
        mean = jnp.mean(gained * h, axis=1, keepdims=True)
        dh_ref[...] = (cot_ref[...].astype(f32) + scale * gained - h * (scale * scale * scale) * mean).astype(bf16)


def final(rd, slot_t, gk_t, dl, router, gain, hidden, cotangent):
    experts, tokens = slot_t.shape
    width = hidden.shape[1]
    chunk = min(32, experts)
    steps = experts // chunk
    return pl.pallas_call(
        final_kernel,
        grid=(steps,),
        in_specs=[
            pl.BlockSpec((chunk * SUB, width), lambda i: (i, 0)),
            pl.BlockSpec((chunk * SUB, width // 4), lambda i: (i, 4)),
            pl.BlockSpec((chunk, tokens), lambda i: (i, 0)),
            pl.BlockSpec((chunk, tokens), lambda i: (i, 0)),
            whole(dl.shape),
            whole(router.shape),
            whole((1, width)),
            whole((tokens, width)),
            whole((tokens, width)),
        ],
        out_specs=whole((tokens, width)),
        out_shape=jax.ShapeDtypeStruct((tokens, width), bf16),
        scratch_shapes=[pltpu.VMEM((tokens, width), f32)],
        compiler_params=params(),
        cost_estimate=pl.CostEstimate(flops=4 * experts * SUB * tokens * width, bytes_accessed=9_000_000, transcendentals=tokens),
    )(rd, rd, slot_t, gk_t, dl, router, gain, hidden, cotangent)


def place_kernel(sums_ref, router_ref, gain_ref):
    experts, n_rows, _ = sums_ref.shape
    rows_each = n_rows - SUB
    received = sums_ref[...].astype(f32)
    router_ref[...] = received[:, :rows_each].reshape(experts * rows_each, MSG)[:, : router_ref.shape[1]]
    gain_ref[...] = jnp.sum(received[:, rows_each:].reshape(gain_ref.shape[0], -1, MSG), axis=1)


def place(received, width, experts):
    return pl.pallas_call(
        place_kernel,
        out_shape=[jax.ShapeDtypeStruct((width, experts), f32), jax.ShapeDtypeStruct((width // MSG, MSG), f32)],
        compiler_params=params(16),
        cost_estimate=pl.CostEstimate(flops=received.size, bytes_accessed=2_000_000, transcendentals=0),
    )(received)


def on_device(hidden, cotangent, norm_gain, router, w_gate, w_up, w_down, expert_ids):
    tokens, width = hidden.shape
    top = expert_ids.shape[1]
    experts = router.shape[1]
    quarter = width // 4
    limit = tokens * top
    gain = norm_gain.reshape(1, width)
    wg, wu, wd = w_gate[0], w_up[0], w_down[0]
    own = width // experts
    extra = quarter + (own // SUB + 1) * MSG

    me = lax.axis_index(AXES)
    router_rows = lax.dynamic_slice_in_dim(router, me * own, own, 0).astype(f32)
    router_rows = jnp.pad(router_rows, ((0, 0), (0, MSG - experts)))
    gain_rows = jnp.broadcast_to(lax.dynamic_slice_in_dim(norm_gain, me * own, own, 0)[:, None], (own, MSG))
    target = lax.broadcasted_iota(jnp.int32, (SUB, MSG), 1) - (me % (MSG // own)) * own

    s1, normed, slot, slot_t = front(hidden, gain, expert_ids.T, experts)
    r1 = exchange(s1.reshape(experts, HI, width + quarter)).reshape(experts * HI, width + quarter)
    gates, s2 = second(normed, cotangent, slot, slot_t, router)
    both, wd_t = turn(wg, wu, wd)
    r2 = exchange(s2.reshape(experts, SUB, width + quarter + MSG)).reshape(experts * SUB, width + quarter + MSG)
    act, fa, fb, x2 = x_side(r1, wg, wu)
    dab, c2, q_msg, scale = c_side(r2, wd_t, act, fa, fb, limit)
    q_home = exchange(q_msg.reshape(experts, 1, MSG)).reshape(experts, MSG)
    back, part = dx_side(dab, both, r1, x2, scale, extra)
    back, dl, gk_t = home(q_home, slot, gates, normed, part, back)
    scale, dl = lax.optimization_barrier((scale, dl))
    d_wgate, d_wup, d_wdown = weight_grads(r1, r2, x2, c2, act, dab, scale)
    rd = exchange(back.reshape(experts, HI, width + extra)).reshape(experts * HI, width + extra)
    d_wgate, gain_rows, router_rows, target = lax.optimization_barrier((d_wgate, gain_rows, router_rows, target))
    message = sums(rd, router_rows, gain_rows, target, experts, width)
    received = exchange(message)
    d_hidden = final(rd, slot_t, gk_t, dl, router, gain, hidden, cotangent)
    d_router, d_gain = place(received, width, experts)
    return (d_hidden, d_gain.reshape(width), d_router, d_wgate[None], d_wup[None], d_wdown[None])


def solution(mesh):
    rows_spec, stack_spec = P(AXES, None), P(AXES, None, None)
    in_specs = (rows_spec, rows_spec, P(), P(), stack_spec, stack_spec, stack_spec, rows_spec)
    out_specs = (rows_spec, P(), P(), stack_spec, stack_spec, stack_spec)
    return jax.shard_map(on_device, mesh=mesh, in_specs=in_specs, out_specs=out_specs, check_vma=False)
```

```python
import functools

import jax
import jax.numpy as jnp
from jax import lax
from jax.experimental import pallas as pl
from jax.experimental.pallas import tpu as pltpu
from jax.sharding import PartitionSpec as P

norm_eps = 1e-06
HI = 8
SUB = 8
MSG = 128
MARK = 128.0
TILE = 256
AXES = ("seq", "exp")
bf16, f32 = jnp.bfloat16, jnp.float32


def params(mib=60):
    return pltpu.CompilerParams(vmem_limit_bytes=mib * 1024 * 1024)


def whole(shape, **kw):
    return pl.BlockSpec(shape, lambda *_: (0,) * len(shape), **kw)


def iota(shape, dim):
    return lax.broadcasted_iota(jnp.int32, shape, dim)


def mm(a, b):
    return jnp.dot(a, b, preferred_element_type=f32)


def mm_nt(a, b):
    return lax.dot_general(a, b, (((1,), (1,)), ((), ())), preferred_element_type=f32)


def mm_tn(a, b):
    return lax.dot_general(a, b, (((0,), (0,)), ((), ())), preferred_element_type=f32)


def exchange(x):
    return lax.all_to_all(x, AXES, split_axis=0, concat_axis=0, tiled=True)


def slots_chosen(slot_t, weight_t=None):
    experts, tokens = slot_t.shape
    which = iota((experts, HI, tokens), 1).astype(f32)
    chosen = jnp.where(slot_t[:, None, :] == which, 1.0 if weight_t is None else weight_t[:, None, :], 0.0)
    return chosen.reshape(experts * HI, tokens).astype(bf16)


def quarter_chosen(slot_t, j, weight_t=None):
    experts, tokens = slot_t.shape
    row = iota((experts, SUB, tokens), 1)
    chosen = (slot_t[:, None, :] == (HI + row // 4).astype(f32)) & (row % 4 == j)
    weight = 1.0 if weight_t is None else weight_t[:, None, :]
    return jnp.where(chosen, weight, 0.0).reshape(experts * SUB, tokens).astype(bf16)


def front_kernel(hid_ref, gain_ref, ids_ref, out_ref, normed_ref, slot_ref, slot_t_ref):
    step = pl.program_id(0)
    tokens, width = hid_ref.shape
    experts = slot_ref.shape[1]
    quarter = width // 4
    chunk = out_ref.shape[0] // HI

    @pl.when(step == 0)
    def _():
        h = hid_ref[...].astype(f32)
        scale = lax.rsqrt(jnp.mean(h * h, axis=1, keepdims=True) + norm_eps)
        normed_ref[...] = (h * scale * gain_ref[...]).astype(bf16)
        ids = ids_ref[...]
        expert = iota((experts, tokens), 0)
        member = jnp.zeros((experts, tokens), f32)
        for k in range(ids.shape[0]):
            member += jnp.where(ids[k : k + 1, :] == expert, 1.0, 0.0)
        earlier = jnp.where(iota((tokens, tokens), 0) < iota((tokens, tokens), 1), 1.0, 0.0)
        position = mm(member.astype(bf16), earlier.astype(bf16))
        slot_t = jnp.where(member > 0.0, position, 99.0)
        slot_ref[...] = slot_t.T
        slot_t_ref[...] = slot_t

    slot_t = slot_t_ref[pl.ds(pl.multiple_of(step * chunk, chunk), chunk), :]
    out_ref[:, :width] = mm(slots_chosen(slot_t), normed_ref[...]).astype(bf16)
    total = mm(quarter_chosen(slot_t, 0), normed_ref[:, :quarter])
    for j in range(1, 4):
        total = total + mm(quarter_chosen(slot_t, j), normed_ref[:, j * quarter : (j + 1) * quarter])
    out_ref[:, width:] = total.astype(bf16)


def front(hidden, gain, ids, experts):
    tokens, width = hidden.shape
    columns = width + width // 4
    chunk = experts // 4
    return pl.pallas_call(
        front_kernel,
        grid=(4,),
        in_specs=[whole((tokens, width)), whole((1, width)), whole(ids.shape)],
        out_specs=[
            pl.BlockSpec((chunk * HI, columns), lambda i: (i, 0)),
            whole((tokens, width)),
            whole((tokens, experts)),
            whole((experts, tokens)),
        ],
        out_shape=[
            jax.ShapeDtypeStruct((experts * HI, columns), bf16),
            jax.ShapeDtypeStruct((tokens, width), bf16),
            jax.ShapeDtypeStruct((tokens, experts), f32),
            jax.ShapeDtypeStruct((experts, tokens), f32),
        ],
        compiler_params=params(),
        cost_estimate=pl.CostEstimate(flops=4 * experts * HI * tokens * width, bytes_accessed=7_000_000, transcendentals=tokens),
    )(hidden, gain, ids)


def second_kernel(normed_ref, cot_ref, slot_ref, slot_t_ref, router_ref, gates_ref, out_ref, tiles, p8, p2, empty):
    step = pl.program_id(0)
    count = tiles.shape[0]
    per = count // 4

    @pl.when(step == 0)
    def _():
        logits = mm(normed_ref[...], router_ref[...])
        weights = jnp.where(slot_ref[...] < 50.0, jnp.exp(logits), 0.0)
        gates = weights / jnp.sum(weights, axis=1, keepdims=True)
        gates_ref[...] = gates
        slot_t = slot_t_ref[...]
        gates_t = gates.astype(bf16).astype(f32).T
        for j in range(count):
            tiles[j] = cot_ref[:, j * MSG : (j + 1) * MSG]
        p8[...] = slots_chosen(slot_t, gates_t)
        first = iota(empty.shape[1:], 1) == 0
        used = jnp.sum(slots_chosen(slot_t).astype(f32), axis=1, keepdims=True)
        empty[0] = jnp.where(first & (used < 0.5), MARK, 0.0)
        for j in range(4):
            p2[j] = quarter_chosen(slot_t, j, gates_t)
        used = sum(jnp.sum(quarter_chosen(slot_t, j).astype(f32), axis=1, keepdims=True) for j in range(4))
        empty[1] = jnp.where(first & (used < 0.5), MARK, 0.0)

    @pl.when(step < count)
    def _():
        mark = jnp.where(step == 0, empty[0], 0.0)
        out_ref[...] = (mm(p8[...], tiles[jnp.minimum(step, count - 1)]) + mark).astype(bf16)

    @pl.when(step >= count)
    def _():
        at = jnp.clip(step - count, 0, per - 1)
        total = mm(p2[0], tiles[at])
        for j in range(1, 4):
            total = total + mm(p2[j], tiles[j * per + at])
        out_ref[...] = (total + jnp.where(step == count, empty[1], 0.0)).astype(bf16)


def second(normed, cotangent, slot, slot_t, router):
    tokens, width = normed.shape
    experts = slot.shape[1]
    count = width // MSG
    steps = count + count // 4
    n_rows = experts * HI
    return pl.pallas_call(
        second_kernel,
        grid=(steps,),
        in_specs=[whole(normed.shape), whole(cotangent.shape), whole(slot.shape), whole(slot_t.shape), whole(router.shape)],
        out_specs=[whole((tokens, experts)), pl.BlockSpec((n_rows, MSG), lambda i: (0, i))],
        out_shape=[
            jax.ShapeDtypeStruct((tokens, experts), f32),
            jax.ShapeDtypeStruct((n_rows, steps * MSG), bf16),
        ],
        scratch_shapes=[
            pltpu.VMEM((count, tokens, MSG), bf16),
            pltpu.VMEM((n_rows, tokens), bf16),
            pltpu.VMEM((4, n_rows, tokens), bf16),
            pltpu.VMEM((2, n_rows, MSG), f32),
        ],
        compiler_params=params(),
        cost_estimate=pl.CostEstimate(flops=4 * n_rows * tokens * width, bytes_accessed=8_000_000, transcendentals=tokens * experts),
    )(normed, cotangent, slot, slot_t, router)


def turn_kernel(wg_ref, wu_ref, wd_ref, both_ref, wd_t_ref):
    both_ref[: wg_ref.shape[1]] = wg_ref[...].T
    both_ref[wg_ref.shape[1] :] = wu_ref[...].T
    wd_t_ref[...] = wd_ref[...].T


def turn(wg, wu, wd):
    width, hid = wg.shape
    tile = min(TILE, hid)
    tall, wide = pl.BlockSpec((width, tile), lambda i: (0, i)), pl.BlockSpec((tile, width), lambda i: (i, 0))
    return pl.pallas_call(
        turn_kernel,
        grid=(hid // tile,),
        in_specs=[tall, tall, wide],
        out_specs=[pl.BlockSpec((2 * tile, width), lambda i: (i, 0)), tall],
        out_shape=[jax.ShapeDtypeStruct((2 * hid, width), bf16), jax.ShapeDtypeStruct((width, hid), bf16)],
        compiler_params=params(),
        cost_estimate=pl.CostEstimate(flops=3 * wg.size, bytes_accessed=19_000_000, transcendentals=0),
    )(wg, wu, wd)


def gather_quarters(ext_ref, target):
    n_rows, quarter = ext_ref.shape
    sources = n_rows // SUB
    chunk = min(32, sources)
    out_rows, in_rows = 2 * chunk, SUB * chunk
    index, column = iota((4 * out_rows, in_rows), 0), iota((4 * out_rows, in_rows), 1)
    pick = jnp.where(column == 4 * (index % out_rows) + index // out_rows, 1.0, 0.0).astype(bf16)
    for j in range(sources // chunk):
        part = mm(pick, ext_ref[j * in_rows : (j + 1) * in_rows, :]).astype(bf16)
        for q in range(4):
            target[j * out_rows : (j + 1) * out_rows, q * quarter : (q + 1) * quarter] = part[q * out_rows : (q + 1) * out_rows]


def x_kernel(x_ref, ext_ref, wg_ref, wu_ref, act_ref, fa_ref, fb_ref, x2_ref, held):
    step = pl.program_id(0)

    @pl.when(step < 4)
    def _():
        held[...] = x_ref[...]

    @pl.when(step == 4)
    def _():
        gather_quarters(ext_ref, held)
        x2_ref[...] = held[...]

    a = mm(held[...], wg_ref[...])
    b = mm(held[...], wu_ref[...])
    s = jax.nn.sigmoid(a)
    act_ref[...] = (a * s * b).astype(bf16)
    fa_ref[...] = (b * s * (1.0 + a * (1.0 - s))).astype(bf16)
    fb_ref[...] = (a * s).astype(bf16)


def x_side(r1, wg, wu):
    width, hid = wg.shape
    main = r1.shape[0]
    block = main // 4
    total = 5 * block
    out = pl.BlockSpec((block, hid), lambda i: (i, 0))
    return pl.pallas_call(
        x_kernel,
        grid=(5,),
        in_specs=[
            pl.BlockSpec((block, width), lambda i: (jnp.minimum(i, 3), 0)),
            pl.BlockSpec((main, width // 4), lambda i: (0, 4)),
            whole(wg.shape),
            whole(wu.shape),
        ],
        out_specs=[out, out, out, whole((block, width))],
        out_shape=[
            jax.ShapeDtypeStruct((total, hid), bf16),
            jax.ShapeDtypeStruct((total, hid), bf16),
            jax.ShapeDtypeStruct((total, hid), bf16),
            jax.ShapeDtypeStruct((block, width), bf16),
        ],
        scratch_shapes=[pltpu.VMEM((block, width), bf16)],
        compiler_params=params(),
        cost_estimate=pl.CostEstimate(flops=4 * total * wg.size, bytes_accessed=24_000_000, transcendentals=total * hid),
    )(r1, r1, wg, wu)


def folded(product):
    total = product[:, :MSG]
    for j in range(1, product.shape[1] // MSG):
        total = total + product[:, j * MSG : (j + 1) * MSG]
    return total


def c_kernel(limit, c_ref, ext_ref, wd_t_ref, act_ref, fa_ref, fb_ref, dab_ref, c2_ref, msg_ref, scale_ref, q8, q2):
    step, last = pl.program_id(0), pl.num_programs(0) - 1
    sources = msg_ref.shape[0]
    main, tail = c_ref.shape[0], c2_ref.shape[0]
    tile = act_ref.shape[1]

    @pl.when(step == 0)
    def _():
        gather_quarters(ext_ref, c2_ref)
        q8[...] = jnp.zeros_like(q8)
        q2[...] = jnp.zeros_like(q2)

    for rows, c, total in ((slice(0, main), c_ref, q8), (slice(main, main + tail), c2_ref, q2)):
        u = mm(c[...], wd_t_ref[...])
        total[...] += folded(act_ref[rows].astype(f32) * u)
        dab_ref[rows, :tile] = (u * fa_ref[rows].astype(f32)).astype(bf16)
        dab_ref[rows, tile:] = (u * fb_ref[rows].astype(f32)).astype(bf16)

    @pl.when(step == last)
    def _():
        lane, which = iota((sources, HI, MSG), 2), iota((sources, HI, MSG), 1)
        gather = jnp.where(iota((sources, tail), 1) // 2 == iota((sources, tail), 0), 1.0, 0.0).astype(bf16)
        own_lane = iota((tail, MSG), 1) == HI + iota((tail, MSG), 0) % 2

        def table(column, tail_column):
            table = jnp.sum(jnp.where(lane == which, column.reshape(sources, HI, 1), 0.0), axis=1)
            return table + mm(gather, jnp.where(own_lane, tail_column, 0.0).astype(bf16))

        def live(ref):
            return jnp.where(ref[:, :MSG].astype(f32)[:, 0:1] < MARK / 2, 1.0, 0.0)

        q_rows = table(jnp.sum(q8[...], axis=1, keepdims=True), jnp.sum(q2[...], axis=1, keepdims=True))
        count = jnp.sum(table(live(c_ref), live(c2_ref)), axis=1, keepdims=True)
        lower = jnp.where(iota((sources, sources), 1) < iota((sources, sources), 0), 1.0, 0.0).astype(bf16)
        offset = mm(lower, jnp.broadcast_to(count, (sources, MSG)).astype(bf16))
        lane = iota((sources, MSG), 1)
        slot = jnp.where(lane < 10, lane, lane - 10).astype(f32)
        kept = (slot < count) & (offset + slot < limit) & (lane < 20)
        msg_ref[...] = jnp.where(kept, jnp.where(lane < 10, q_rows, 1.0), 0.0)
        scale_ref[...] = jnp.where(kept & (lane < 10), 1.0, 0.0).astype(bf16)


def c_side(r2, wd_t, act, fa, fb, limit):
    width, hid = wd_t.shape
    main = r2.shape[0]
    sources, tail = main // SUB, main // 4
    total = main + tail
    tile = min(TILE, hid)

    def columns(n_rows, n_columns):
        return pl.BlockSpec((n_rows, n_columns), lambda i: (0, i))

    return pl.pallas_call(
        functools.partial(c_kernel, float(limit)),
        grid=(hid // tile,),
        in_specs=[
            whole((main, width)),
            pl.BlockSpec((main, width // 4), lambda i: (0, 4)),
            columns(width, tile),
            columns(total, tile),
            columns(total, tile),
            columns(total, tile),
        ],
        out_specs=[columns(total, 2 * tile), whole((tail, width)), whole((sources, MSG)), whole((sources, MSG))],
        out_shape=[
            jax.ShapeDtypeStruct((total, 2 * hid), bf16),
            jax.ShapeDtypeStruct((tail, width), bf16),
            jax.ShapeDtypeStruct((sources, MSG), f32),
            jax.ShapeDtypeStruct((sources, MSG), bf16),
        ],
        scratch_shapes=[pltpu.VMEM((main, MSG), f32), pltpu.VMEM((tail, MSG), f32)],
        compiler_params=params(),
        cost_estimate=pl.CostEstimate(flops=2 * total * wd_t.size, bytes_accessed=20_000_000, transcendentals=0),
    )(r2, r2, wd_t, act, fa, fb)


def column_of(table):
    sources = table.shape[0]
    lane, which = iota((sources, HI, MSG), 2), iota((sources, HI, MSG), 1)
    spread = jnp.where(lane == which, table[:, None, :], 0.0)
    return jnp.sum(spread.reshape(sources * HI, MSG), axis=1, keepdims=True)


def tail_column_of(table):
    sources = table.shape[0]
    total = 2 * sources
    scatter = jnp.where(iota((total, sources), 0) // 2 == iota((total, sources), 1), 1.0, 0.0).astype(bf16)
    lane = HI + iota((total, MSG), 0) % 2
    return jnp.sum(jnp.where(iota((total, MSG), 1) == lane, mm(scatter, table), 0.0), axis=1, keepdims=True)


def dx_kernel(dab_ref, both_ref, x_ref, x2_ref, scale_ref, out_ref, part_ref, ext, s8, s2):
    step = pl.program_id(0)
    sources = scale_ref.shape[0]
    main, quarter = out_ref.shape

    @pl.when(step == 0)
    def _():
        table = scale_ref[...]
        s8[...] = jnp.broadcast_to(column_of(table.astype(f32)), s8.shape)
        s2[...] = jnp.broadcast_to(tail_column_of(table), s2.shape)
        ext[...] = jnp.zeros_like(ext)

    @pl.when(step < 4)
    def _():
        dx = mm(dab_ref[...], both_ref[...])
        rounded = dx.astype(bf16)
        out_ref[...] = rounded[:main]
        chunk = min(32, sources)
        n_rows = SUB * chunk
        pick = jnp.where(iota((n_rows, 2 * chunk), 0) == 4 * iota((n_rows, 2 * chunk), 1) + step, 1.0, 0.0).astype(bf16)
        for j in range(sources // chunk):
            tail = rounded[main + j * 2 * chunk : main + (j + 1) * 2 * chunk]
            ext[j * n_rows : (j + 1) * n_rows, :] += mm(pick, tail).astype(bf16)
        part = jnp.sum(x_ref[...].astype(f32) * dx[:main] * s8[:, 0:1], axis=0, keepdims=True)
        part = part + jnp.sum(x2_ref[...].astype(f32) * dx[main:] * s2[:, 0:1], axis=0, keepdims=True)
        column = jnp.concatenate(
            [jnp.broadcast_to(part[:, j : j + MSG], (MSG, MSG)).T for j in range(0, quarter, MSG)], axis=0
        )
        dests = part_ref.shape[0] // SUB
        groups = quarter // dests // SUB
        column = column.reshape(dests, groups, SUB, MSG)
        lane = iota((dests, SUB, MSG), 2)
        spread = jnp.zeros((dests, SUB, MSG), f32)
        for g in range(groups):
            spread = jnp.where(lane == g, column[:, g], spread)
        part_ref[...] = spread.reshape(dests * SUB, MSG).astype(bf16)

    @pl.when(step == 4)
    def _():
        out_ref[...] = ext[...]


def dx_side(dab, both, r1, x2, scale, extra):
    sources = scale.shape[0]
    twice, width = both.shape
    quarter = width // 4
    main, total = sources * HI, 2 * sources

    def columns(n_rows):
        return pl.BlockSpec((n_rows, quarter), lambda i: (0, jnp.minimum(i, 3)))

    return pl.pallas_call(
        dx_kernel,
        grid=(5,),
        in_specs=[whole(dab.shape), columns(twice), columns(main), columns(total), whole(scale.shape)],
        out_specs=[
            pl.BlockSpec((main, quarter), lambda i: (0, i)),
            pl.BlockSpec((main // 4, MSG), lambda i: (jnp.minimum(i, 3), 0)),
        ],
        out_shape=[jax.ShapeDtypeStruct((main, width + extra), bf16), jax.ShapeDtypeStruct((main, MSG), bf16)],
        scratch_shapes=[pltpu.VMEM((main, quarter), bf16), pltpu.VMEM((main, MSG), f32), pltpu.VMEM((total, MSG), f32)],
        compiler_params=params(),
        cost_estimate=pl.CostEstimate(flops=2 * (main + total) * both.size, bytes_accessed=20_000_000, transcendentals=0),
    )(dab, both, r1, x2, scale)


def weights_kernel(x_ref, c_ref, x2_ref, c2_ref, act_ref, dab_ref, scale_ref, dwg_ref, dwu_ref, dwd_ref, act_s, dab_s):
    main = x_ref.shape[0]
    hid = act_ref.shape[1]
    tile = min(TILE, hid)

    @pl.when(pl.program_id(0) == 0)
    def _():
        table = scale_ref[...]
        column, tail_column = column_of(table.astype(f32)), tail_column_of(table)
        for source, target in ((act_ref, act_s), (dab_ref, dab_s)):
            target[:main] = (source[:main].astype(f32) * column).astype(bf16)
            target[main:] = (source[main:].astype(f32) * tail_column).astype(bf16)

    both = (mm_tn(x_ref[...], dab_s[:main]) + mm_tn(x2_ref[...], dab_s[main:])).astype(bf16)
    for j in range(hid // tile):
        dwg_ref[:, j * tile : (j + 1) * tile] = both[:, 2 * j * tile : (2 * j + 1) * tile]
        dwu_ref[:, j * tile : (j + 1) * tile] = both[:, (2 * j + 1) * tile : (2 * j + 2) * tile]
    dwd_ref[...] = (mm_tn(act_s[:main], c_ref[...]) + mm_tn(act_s[main:], c2_ref[...])).astype(bf16)


def weight_grads(r1, r2, x2, c2, act, dab, scale):
    total, hid = act.shape
    main, width = r1.shape[0], x2.shape[1]
    tile = min(256, width)
    steps = width // tile

    def columns(n_rows):
        return pl.BlockSpec((n_rows, tile), lambda i: (0, i))

    return pl.pallas_call(
        weights_kernel,
        grid=(steps,),
        in_specs=[columns(main), columns(main), columns(total - main), columns(total - main)]
        + [whole(act.shape), whole(dab.shape), whole(scale.shape)],
        out_specs=[pl.BlockSpec((tile, hid), lambda i: (i, 0)), pl.BlockSpec((tile, hid), lambda i: (i, 0)), columns(hid)],
        out_shape=[
            jax.ShapeDtypeStruct((width, hid), bf16),
            jax.ShapeDtypeStruct((width, hid), bf16),
            jax.ShapeDtypeStruct((hid, width), bf16),
        ],
        scratch_shapes=[pltpu.VMEM(act.shape, bf16), pltpu.VMEM(dab.shape, bf16)],
        compiler_params=params(),
        cost_estimate=pl.CostEstimate(flops=6 * total * width * hid, bytes_accessed=36_000_000, transcendentals=0),
    )(r1, r2, x2, c2, act, dab, scale)


def home_kernel(q_ref, slot_ref, gates_ref, normed_ref, part_ref, _, back_ref, dl_ref, gk_t_ref, router_part):
    step, last = pl.program_id(0), pl.num_programs(0) - 1
    experts = q_ref.shape[0]

    @pl.when(step == 0)
    def _():
        q_t = q_ref[...].T
        slot, gates = slot_ref[...], gates_ref[...]
        gated = jnp.zeros_like(gates)
        kept = jnp.zeros_like(gates)
        for s in range(10):
            here = slot == s
            gated = gated + jnp.where(here, q_t[s : s + 1, :], 0.0)
            kept = kept + jnp.where(here, q_t[10 + s : 11 + s, :], 0.0)
        rounded = gates.astype(bf16).astype(f32)
        gated = gated * jnp.where(rounded > 0.0, gates / jnp.where(rounded > 0.0, rounded, 1.0), 0.0)
        dsel = gated - gates * jnp.sum(gated, axis=1, keepdims=True)
        dl = dsel.astype(bf16)
        dl_ref[...] = dl
        gk_t_ref[...] = kept.T
        if experts < MSG:
            dl = jnp.concatenate([dl, jnp.zeros((dl.shape[0], MSG - experts), bf16)], axis=1)
        groups = router_part.shape[0]
        partial = mm_tn(normed_ref[...], dl).reshape(experts, groups, SUB, MSG)
        for g in range(groups):
            router_part[g] = partial[:, g].reshape(experts * SUB, MSG).astype(bf16)

    @pl.when(step < last)
    def _():
        back_ref[...] = router_part[jnp.minimum(step, router_part.shape[0] - 1)]

    @pl.when(step == last)
    def _():
        back_ref[...] = part_ref[...]


def home(q, slot, gates, normed, part, back):
    tokens, experts = slot.shape
    width = normed.shape[1]
    groups = width // experts // SUB
    first = (width + width // 4) // MSG
    return pl.pallas_call(
        home_kernel,
        grid=(groups + 1,),
        in_specs=[whole(q.shape), whole(slot.shape), whole(gates.shape), whole(normed.shape), whole(part.shape), pl.BlockSpec(memory_space=pl.ANY)],
        out_specs=[pl.BlockSpec((experts * SUB, MSG), lambda i: (0, first + i)), whole((tokens, experts)), whole((experts, tokens))],
        out_shape=[
            jax.ShapeDtypeStruct(back.shape, bf16),
            jax.ShapeDtypeStruct((tokens, experts), bf16),
            jax.ShapeDtypeStruct((experts, tokens), f32),
        ],
        scratch_shapes=[pltpu.VMEM((groups, experts * SUB, MSG), bf16)],
        input_output_aliases={5: 0},
        compiler_params=params(),
        cost_estimate=pl.CostEstimate(flops=2 * tokens * MSG * width, bytes_accessed=2_500_000, transcendentals=0),
    )(q, slot, gates, normed, part, back)


def sums_kernel(*refs):
    *parts, gain_ref, router_ref, gain_rows_ref, target_ref, out_ref = refs
    copies, n_rows, _ = out_ref.shape
    target = target_ref[...]
    row = iota(target.shape, 0)
    gain_parts = jnp.sum(gain_ref[...].astype(f32).reshape(copies, SUB, MSG), axis=0)
    pieces = []
    placed = jnp.zeros(target.shape, f32)
    for g, ref in enumerate(parts):
        piece = jnp.sum(ref[...].astype(f32).reshape(copies, SUB, MSG), axis=0)
        pieces.append(piece)
        own = slice(g * SUB, (g + 1) * SUB)
        value = gain_parts[:, g : g + 1] + jnp.sum(router_ref[own] * piece, axis=1, keepdims=True)
        placed = jnp.where(target == g * SUB + row, value / gain_rows_ref[own], placed)
    message = jnp.concatenate(pieces + [placed], axis=0)
    out_ref[...] = jnp.broadcast_to(message[None], out_ref.shape).astype(bf16)


def sums(rd, router_rows, gain_rows, target, experts, width):
    groups = width // experts // SUB
    first = (width + width // 4) // MSG
    block = (experts * SUB, MSG)
    specs = [pl.BlockSpec(block, functools.partial(lambda g, i: (0, first + g), g)) for g in range(groups + 1)]
    return pl.pallas_call(
        sums_kernel,
        grid=(1,),
        in_specs=specs + [whole(router_rows.shape), whole(gain_rows.shape), whole(target.shape)],
        out_specs=whole((experts, (groups + 1) * SUB, MSG)),
        out_shape=jax.ShapeDtypeStruct((experts, (groups + 1) * SUB, MSG), bf16),
        compiler_params=params(),
        cost_estimate=pl.CostEstimate(flops=experts * SUB * MSG * 8, bytes_accessed=2_000_000, transcendentals=0),
    )(*[rd] * (groups + 1), router_rows, gain_rows, target)


def final_kernel(dx_ref, ext_ref, slot_t_ref, gk_t_ref, dl_ref, router_ref, gain_ref, hid_ref, cot_ref, dh_ref, total):
    step, last = pl.program_id(0), pl.num_programs(0) - 1
    chunk, tokens = slot_t_ref.shape
    n_rows = chunk * SUB
    quarter = ext_ref.shape[1]
    slot, gk = slot_t_ref[...][:, None, :], gk_t_ref[...][:, None, :]
    which = iota((chunk, SUB, tokens), 1)

    def weights(mask):
        return jnp.where(mask, gk, 0.0).reshape(n_rows, tokens).astype(bf16)

    @pl.when(step == 0)
    def _():
        total[...] = mm_nt(dl_ref[...], router_ref[...])

    total[...] += mm_tn(weights(slot == which.astype(f32)), dx_ref[...])
    in_tail = slot == (HI + which // 4).astype(f32)
    for j in range(4):
        total[:, j * quarter : (j + 1) * quarter] += mm_tn(weights(in_tail & (which % 4 == j)), ext_ref[...])

    @pl.when(step == last)
    def _():
        h = hid_ref[...].astype(f32)
        scale = lax.rsqrt(jnp.mean(h * h, axis=1, keepdims=True) + norm_eps)
        gained = gain_ref[...] * total[...]
        mean = jnp.mean(gained * h, axis=1, keepdims=True)
        dh_ref[...] = (cot_ref[...].astype(f32) + scale * gained - h * (scale * scale * scale) * mean).astype(bf16)


def final(rd, slot_t, gk_t, dl, router, gain, hidden, cotangent):
    experts, tokens = slot_t.shape
    width = hidden.shape[1]
    chunk = min(32, experts)
    steps = experts // chunk
    return pl.pallas_call(
        final_kernel,
        grid=(steps,),
        in_specs=[
            pl.BlockSpec((chunk * SUB, width), lambda i: (i, 0)),
            pl.BlockSpec((chunk * SUB, width // 4), lambda i: (i, 4)),
            pl.BlockSpec((chunk, tokens), lambda i: (i, 0)),
            pl.BlockSpec((chunk, tokens), lambda i: (i, 0)),
            whole(dl.shape),
            whole(router.shape),
            whole((1, width)),
            whole((tokens, width)),
            whole((tokens, width)),
        ],
        out_specs=whole((tokens, width)),
        out_shape=jax.ShapeDtypeStruct((tokens, width), bf16),
        scratch_shapes=[pltpu.VMEM((tokens, width), f32)],
        compiler_params=params(),
        cost_estimate=pl.CostEstimate(flops=4 * experts * SUB * tokens * width, bytes_accessed=9_000_000, transcendentals=tokens),
    )(rd, rd, slot_t, gk_t, dl, router, gain, hidden, cotangent)


def place_kernel(sums_ref, router_ref, gain_ref):
    experts, n_rows, _ = sums_ref.shape
    rows_each = n_rows - SUB
    received = sums_ref[...].astype(f32)
    router_ref[...] = received[:, :rows_each].reshape(experts * rows_each, MSG)[:, : router_ref.shape[1]]
    gain_ref[...] = jnp.sum(received[:, rows_each:].reshape(gain_ref.shape[0], -1, MSG), axis=1)


def place(received, width, experts):
    return pl.pallas_call(
        place_kernel,
        out_shape=[jax.ShapeDtypeStruct((width, experts), f32), jax.ShapeDtypeStruct((width // MSG, MSG), f32)],
        compiler_params=params(16),
        cost_estimate=pl.CostEstimate(flops=received.size, bytes_accessed=2_000_000, transcendentals=0),
    )(received)


def on_device(hidden, cotangent, norm_gain, router, w_gate, w_up, w_down, expert_ids):
    tokens, width = hidden.shape
    top = expert_ids.shape[1]
    experts = router.shape[1]
    quarter = width // 4
    limit = tokens * top
    gain = norm_gain.reshape(1, width)
    wg, wu, wd = w_gate[0], w_up[0], w_down[0]
    own = width // experts
    extra = quarter + (own // SUB + 1) * MSG

    me = lax.axis_index(AXES)
    router_rows = lax.dynamic_slice_in_dim(router, me * own, own, 0).astype(f32)
    router_rows = jnp.pad(router_rows, ((0, 0), (0, MSG - experts)))
    gain_rows = jnp.broadcast_to(lax.dynamic_slice_in_dim(norm_gain, me * own, own, 0)[:, None], (own, MSG))
    target = lax.broadcasted_iota(jnp.int32, (SUB, MSG), 1) - (me % (MSG // own)) * own

    s1, normed, slot, slot_t = front(hidden, gain, expert_ids.T, experts)
    r1 = exchange(s1.reshape(experts, HI, width + quarter)).reshape(experts * HI, width + quarter)
    gates, s2 = second(normed, cotangent, slot, slot_t, router)
    both, wd_t = turn(wg, wu, wd)
    r2 = exchange(s2.reshape(experts, SUB, width + quarter)).reshape(experts * SUB, width + quarter)
    act, fa, fb, x2 = x_side(r1, wg, wu)
    dab, c2, q_msg, scale = c_side(r2, wd_t, act, fa, fb, limit)
    q_home = exchange(q_msg.reshape(experts, 1, MSG)).reshape(experts, MSG)
    back, part = dx_side(dab, both, r1, x2, scale, extra)
    back, dl, gk_t = home(q_home, slot, gates, normed, part, back)
    scale, dl = lax.optimization_barrier((scale, dl))
    d_wgate, d_wup, d_wdown = weight_grads(r1, r2, x2, c2, act, dab, scale)
    rd = exchange(back.reshape(experts, HI, width + extra)).reshape(experts * HI, width + extra)
    d_wgate, gain_rows, router_rows, target = lax.optimization_barrier((d_wgate, gain_rows, router_rows, target))
    message = sums(rd, router_rows, gain_rows, target, experts, width)
    received = exchange(message)
    d_hidden = final(rd, slot_t, gk_t, dl, router, gain, hidden, cotangent)
    d_router, d_gain = place(received, width, experts)
    return (d_hidden, d_gain.reshape(width), d_router, d_wgate[None], d_wup[None], d_wdown[None])


def solution(mesh):
    rows_spec, stack_spec = P(AXES, None), P(AXES, None, None)
    in_specs = (rows_spec, rows_spec, P(), P(), stack_spec, stack_spec, stack_spec, rows_spec)
    out_specs = (rows_spec, P(), P(), stack_spec, stack_spec, stack_spec)
    return jax.shard_map(on_device, mesh=mesh, in_specs=in_specs, out_specs=out_specs, check_vma=False)
```

```python
import functools

import jax
import jax.numpy as jnp
from jax import lax
from jax.experimental import pallas as pl
from jax.experimental.pallas import tpu as pltpu
from jax.sharding import PartitionSpec as P

norm_eps = 1e-06
HI = 8
SUB = 8
MSG = 128
MARK = 128.0
TILE = 256
AXES = ("seq", "exp")
bf16, f32 = jnp.bfloat16, jnp.float32


def params(mib=60):
    return pltpu.CompilerParams(vmem_limit_bytes=mib * 1024 * 1024)


def whole(shape, **kw):
    return pl.BlockSpec(shape, lambda *_: (0,) * len(shape), **kw)


def iota(shape, dim):
    return lax.broadcasted_iota(jnp.int32, shape, dim)


def mm(a, b):
    return jnp.dot(a, b, preferred_element_type=f32)


def mm_nt(a, b):
    return lax.dot_general(a, b, (((1,), (1,)), ((), ())), preferred_element_type=f32)


def mm_tn(a, b):
    return lax.dot_general(a, b, (((0,), (0,)), ((), ())), preferred_element_type=f32)


def exchange(x):
    return lax.all_to_all(x, AXES, split_axis=0, concat_axis=0, tiled=True)


def slots_chosen(slot_t, weight_t=None):
    experts, tokens = slot_t.shape
    which = iota((experts, HI, tokens), 1).astype(f32)
    chosen = jnp.where(slot_t[:, None, :] == which, 1.0 if weight_t is None else weight_t[:, None, :], 0.0)
    return chosen.reshape(experts * HI, tokens).astype(bf16)


def quarter_chosen(slot_t, j, weight_t=None):
    experts, tokens = slot_t.shape
    row = iota((experts, SUB, tokens), 1)
    chosen = (slot_t[:, None, :] == (HI + row // 4).astype(f32)) & (row % 4 == j)
    weight = 1.0 if weight_t is None else weight_t[:, None, :]
    return jnp.where(chosen, weight, 0.0).reshape(experts * SUB, tokens).astype(bf16)


def front_kernel(hid_ref, gain_ref, ids_ref, out_ref, normed_ref, slot_ref, slot_t_ref):
    step = pl.program_id(0)
    tokens, width = hid_ref.shape
    experts = slot_ref.shape[1]
    quarter = width // 4
    chunk = out_ref.shape[0] // HI

    @pl.when(step == 0)
    def _():
        h = hid_ref[...].astype(f32)
        scale = lax.rsqrt(jnp.mean(h * h, axis=1, keepdims=True) + norm_eps)
        normed_ref[...] = (h * scale * gain_ref[...]).astype(bf16)
        ids = ids_ref[...]
        expert = iota((experts, tokens), 0)
        member = jnp.zeros((experts, tokens), f32)
        for k in range(ids.shape[0]):
            member += jnp.where(ids[k : k + 1, :] == expert, 1.0, 0.0)
        earlier = jnp.where(iota((tokens, tokens), 0) < iota((tokens, tokens), 1), 1.0, 0.0)
        position = mm(member.astype(bf16), earlier.astype(bf16))
        slot_t = jnp.where(member > 0.0, position, 99.0)
        slot_ref[...] = slot_t.T
        slot_t_ref[...] = slot_t

    slot_t = slot_t_ref[pl.ds(pl.multiple_of(step * chunk, chunk), chunk), :]
    out_ref[:, :width] = mm(slots_chosen(slot_t), normed_ref[...]).astype(bf16)
    total = mm(quarter_chosen(slot_t, 0), normed_ref[:, :quarter])
    for j in range(1, 4):
        total = total + mm(quarter_chosen(slot_t, j), normed_ref[:, j * quarter : (j + 1) * quarter])
    out_ref[:, width:] = total.astype(bf16)


def front(hidden, gain, ids, experts):
    tokens, width = hidden.shape
    columns = width + width // 4
    chunk = experts // 8
    return pl.pallas_call(
        front_kernel,
        grid=(8,),
        in_specs=[whole((tokens, width)), whole((1, width)), whole(ids.shape)],
        out_specs=[
            pl.BlockSpec((chunk * HI, columns), lambda i: (i, 0)),
            whole((tokens, width)),
            whole((tokens, experts)),
            whole((experts, tokens)),
        ],
        out_shape=[
            jax.ShapeDtypeStruct((experts * HI, columns), bf16),
            jax.ShapeDtypeStruct((tokens, width), bf16),
            jax.ShapeDtypeStruct((tokens, experts), f32),
            jax.ShapeDtypeStruct((experts, tokens), f32),
        ],
        compiler_params=params(),
        cost_estimate=pl.CostEstimate(flops=4 * experts * HI * tokens * width, bytes_accessed=7_000_000, transcendentals=tokens),
    )(hidden, gain, ids)


def second_kernel(normed_ref, cot_ref, slot_ref, slot_t_ref, router_ref, gates_ref, out_ref, tiles, p8, p2, empty):
    step = pl.program_id(0)
    count = tiles.shape[0]
    per = count // 4

    @pl.when(step == 0)
    def _():
        logits = mm(normed_ref[...], router_ref[...])
        weights = jnp.where(slot_ref[...] < 50.0, jnp.exp(logits), 0.0)
        gates = weights / jnp.sum(weights, axis=1, keepdims=True)
        gates_ref[...] = gates
        slot_t = slot_t_ref[...]
        gates_t = gates.astype(bf16).astype(f32).T
        for j in range(count):
            tiles[j] = cot_ref[:, j * MSG : (j + 1) * MSG]
        p8[...] = slots_chosen(slot_t, gates_t)
        first = iota(empty.shape[1:], 1) == 0
        used = jnp.sum(slots_chosen(slot_t).astype(f32), axis=1, keepdims=True)
        empty[0] = jnp.where(first & (used < 0.5), MARK, 0.0)
        for j in range(4):
            p2[j] = quarter_chosen(slot_t, j, gates_t)
        used = sum(jnp.sum(quarter_chosen(slot_t, j).astype(f32), axis=1, keepdims=True) for j in range(4))
        empty[1] = jnp.where(first & (used < 0.5), MARK, 0.0)

    @pl.when(step < count)
    def _():
        mark = jnp.where(step == 0, empty[0], 0.0)
        out_ref[...] = (mm(p8[...], tiles[jnp.minimum(step, count - 1)]) + mark).astype(bf16)

    @pl.when(step >= count)
    def _():
        at = jnp.clip(step - count, 0, per - 1)
        total = mm(p2[0], tiles[at])
        for j in range(1, 4):
            total = total + mm(p2[j], tiles[j * per + at])
        out_ref[...] = (total + jnp.where(step == count, empty[1], 0.0)).astype(bf16)


def second(normed, cotangent, slot, slot_t, router):
    tokens, width = normed.shape
    experts = slot.shape[1]
    count = width // MSG
    steps = count + count // 4
    n_rows = experts * HI
    return pl.pallas_call(
        second_kernel,
        grid=(steps,),
        in_specs=[whole(normed.shape), whole(cotangent.shape), whole(slot.shape), whole(slot_t.shape), whole(router.shape)],
        out_specs=[whole((tokens, experts)), pl.BlockSpec((n_rows, MSG), lambda i: (0, i))],
        out_shape=[
            jax.ShapeDtypeStruct((tokens, experts), f32),
            jax.ShapeDtypeStruct((n_rows, steps * MSG), bf16),
        ],
        scratch_shapes=[
            pltpu.VMEM((count, tokens, MSG), bf16),
            pltpu.VMEM((n_rows, tokens), bf16),
            pltpu.VMEM((4, n_rows, tokens), bf16),
            pltpu.VMEM((2, n_rows, MSG), f32),
        ],
        compiler_params=params(),
        cost_estimate=pl.CostEstimate(flops=4 * n_rows * tokens * width, bytes_accessed=8_000_000, transcendentals=tokens * experts),
    )(normed, cotangent, slot, slot_t, router)


def turn_kernel(wg_ref, wu_ref, wd_ref, both_ref, wd_t_ref):
    both_ref[: wg_ref.shape[1]] = wg_ref[...].T
    both_ref[wg_ref.shape[1] :] = wu_ref[...].T
    wd_t_ref[...] = wd_ref[...].T


def turn(wg, wu, wd):
    width, hid = wg.shape
    tile = min(TILE, hid)
    tall, wide = pl.BlockSpec((width, tile), lambda i: (0, i)), pl.BlockSpec((tile, width), lambda i: (i, 0))
    return pl.pallas_call(
        turn_kernel,
        grid=(hid // tile,),
        in_specs=[tall, tall, wide],
        out_specs=[pl.BlockSpec((2 * tile, width), lambda i: (i, 0)), tall],
        out_shape=[jax.ShapeDtypeStruct((2 * hid, width), bf16), jax.ShapeDtypeStruct((width, hid), bf16)],
        compiler_params=params(),
        cost_estimate=pl.CostEstimate(flops=3 * wg.size, bytes_accessed=19_000_000, transcendentals=0),
    )(wg, wu, wd)


def gather_quarters(ext_ref, target):
    n_rows, quarter = ext_ref.shape
    sources = n_rows // SUB
    chunk = min(32, sources)
    out_rows, in_rows = 2 * chunk, SUB * chunk
    index, column = iota((4 * out_rows, in_rows), 0), iota((4 * out_rows, in_rows), 1)
    pick = jnp.where(column == 4 * (index % out_rows) + index // out_rows, 1.0, 0.0).astype(bf16)
    for j in range(sources // chunk):
        part = mm(pick, ext_ref[j * in_rows : (j + 1) * in_rows, :]).astype(bf16)
        for q in range(4):
            target[j * out_rows : (j + 1) * out_rows, q * quarter : (q + 1) * quarter] = part[q * out_rows : (q + 1) * out_rows]


def x_kernel(x_ref, ext_ref, wg_ref, wu_ref, act_ref, fa_ref, fb_ref, x2_ref, held):
    step = pl.program_id(0)

    @pl.when(step < 4)
    def _():
        held[...] = x_ref[...]

    @pl.when(step == 4)
    def _():
        gather_quarters(ext_ref, held)
        x2_ref[...] = held[...]

    a = mm(held[...], wg_ref[...])
    b = mm(held[...], wu_ref[...])
    s = jax.nn.sigmoid(a)
    act_ref[...] = (a * s * b).astype(bf16)
    fa_ref[...] = (b * s * (1.0 + a * (1.0 - s))).astype(bf16)
    fb_ref[...] = (a * s).astype(bf16)


def x_side(r1, wg, wu):
    width, hid = wg.shape
    main = r1.shape[0]
    block = main // 4
    total = 5 * block
    out = pl.BlockSpec((block, hid), lambda i: (i, 0))
    return pl.pallas_call(
        x_kernel,
        grid=(5,),
        in_specs=[
            pl.BlockSpec((block, width), lambda i: (jnp.minimum(i, 3), 0)),
            pl.BlockSpec((main, width // 4), lambda i: (0, 4)),
            whole(wg.shape),
            whole(wu.shape),
        ],
        out_specs=[out, out, out, whole((block, width))],
        out_shape=[
            jax.ShapeDtypeStruct((total, hid), bf16),
            jax.ShapeDtypeStruct((total, hid), bf16),
            jax.ShapeDtypeStruct((total, hid), bf16),
            jax.ShapeDtypeStruct((block, width), bf16),
        ],
        scratch_shapes=[pltpu.VMEM((block, width), bf16)],
        compiler_params=params(),
        cost_estimate=pl.CostEstimate(flops=4 * total * wg.size, bytes_accessed=24_000_000, transcendentals=total * hid),
    )(r1, r1, wg, wu)


def folded(product):
    total = product[:, :MSG]
    for j in range(1, product.shape[1] // MSG):
        total = total + product[:, j * MSG : (j + 1) * MSG]
    return total


def c_kernel(limit, c_ref, ext_ref, wd_t_ref, act_ref, fa_ref, fb_ref, dab_ref, c2_ref, msg_ref, scale_ref, q8, q2):
    step, last = pl.program_id(0), pl.num_programs(0) - 1
    sources = msg_ref.shape[0]
    main, tail = c_ref.shape[0], c2_ref.shape[0]
    tile = act_ref.shape[1]

    @pl.when(step == 0)
    def _():
        gather_quarters(ext_ref, c2_ref)
        q8[...] = jnp.zeros_like(q8)
        q2[...] = jnp.zeros_like(q2)

    for rows, c, total in ((slice(0, main), c_ref, q8), (slice(main, main + tail), c2_ref, q2)):
        u = mm(c[...], wd_t_ref[...])
        total[...] += folded(act_ref[rows].astype(f32) * u)
        dab_ref[rows, :tile] = (u * fa_ref[rows].astype(f32)).astype(bf16)
        dab_ref[rows, tile:] = (u * fb_ref[rows].astype(f32)).astype(bf16)

    @pl.when(step == last)
    def _():
        lane, which = iota((sources, HI, MSG), 2), iota((sources, HI, MSG), 1)
        gather = jnp.where(iota((sources, tail), 1) // 2 == iota((sources, tail), 0), 1.0, 0.0).astype(bf16)
        own_lane = iota((tail, MSG), 1) == HI + iota((tail, MSG), 0) % 2

        def table(column, tail_column):
            table = jnp.sum(jnp.where(lane == which, column.reshape(sources, HI, 1), 0.0), axis=1)
            return table + mm(gather, jnp.where(own_lane, tail_column, 0.0).astype(bf16))

        def live(ref):
            return jnp.where(ref[:, :MSG].astype(f32)[:, 0:1] < MARK / 2, 1.0, 0.0)

        q_rows = table(jnp.sum(q8[...], axis=1, keepdims=True), jnp.sum(q2[...], axis=1, keepdims=True))
        count = jnp.sum(table(live(c_ref), live(c2_ref)), axis=1, keepdims=True)
        lower = jnp.where(iota((sources, sources), 1) < iota((sources, sources), 0), 1.0, 0.0).astype(bf16)
        offset = mm(lower, jnp.broadcast_to(count, (sources, MSG)).astype(bf16))
        lane = iota((sources, MSG), 1)
        slot = jnp.where(lane < 10, lane, lane - 10).astype(f32)
        kept = (slot < count) & (offset + slot < limit) & (lane < 20)
        msg_ref[...] = jnp.where(kept, jnp.where(lane < 10, q_rows, 1.0), 0.0)
        scale_ref[...] = jnp.where(kept & (lane < 10), 1.0, 0.0).astype(bf16)


def c_side(r2, wd_t, act, fa, fb, limit):
    width, hid = wd_t.shape
    main = r2.shape[0]
    sources, tail = main // SUB, main // 4
    total = main + tail
    tile = min(TILE, hid)

    def columns(n_rows, n_columns):
        return pl.BlockSpec((n_rows, n_columns), lambda i: (0, i))

    return pl.pallas_call(
        functools.partial(c_kernel, float(limit)),
        grid=(hid // tile,),
        in_specs=[
            whole((main, width)),
            pl.BlockSpec((main, width // 4), lambda i: (0, 4)),
            columns(width, tile),
            columns(total, tile),
            columns(total, tile),
            columns(total, tile),
        ],
        out_specs=[columns(total, 2 * tile), whole((tail, width)), whole((sources, MSG)), whole((sources, MSG))],
        out_shape=[
            jax.ShapeDtypeStruct((total, 2 * hid), bf16),
            jax.ShapeDtypeStruct((tail, width), bf16),
            jax.ShapeDtypeStruct((sources, MSG), f32),
            jax.ShapeDtypeStruct((sources, MSG), bf16),
        ],
        scratch_shapes=[pltpu.VMEM((main, MSG), f32), pltpu.VMEM((tail, MSG), f32)],
        compiler_params=params(),
        cost_estimate=pl.CostEstimate(flops=2 * total * wd_t.size, bytes_accessed=20_000_000, transcendentals=0),
    )(r2, r2, wd_t, act, fa, fb)


def column_of(table):
    sources = table.shape[0]
    lane, which = iota((sources, HI, MSG), 2), iota((sources, HI, MSG), 1)
    spread = jnp.where(lane == which, table[:, None, :], 0.0)
    return jnp.sum(spread.reshape(sources * HI, MSG), axis=1, keepdims=True)


def tail_column_of(table):
    sources = table.shape[0]
    total = 2 * sources
    scatter = jnp.where(iota((total, sources), 0) // 2 == iota((total, sources), 1), 1.0, 0.0).astype(bf16)
    lane = HI + iota((total, MSG), 0) % 2
    return jnp.sum(jnp.where(iota((total, MSG), 1) == lane, mm(scatter, table), 0.0), axis=1, keepdims=True)


def dx_kernel(dab_ref, both_ref, x_ref, x2_ref, scale_ref, out_ref, part_ref, ext, s8, s2):
    step = pl.program_id(0)
    sources = scale_ref.shape[0]
    main, quarter = out_ref.shape

    @pl.when(step == 0)
    def _():
        table = scale_ref[...]
        s8[...] = jnp.broadcast_to(column_of(table.astype(f32)), s8.shape)
        s2[...] = jnp.broadcast_to(tail_column_of(table), s2.shape)

    @pl.when(step < 4)
    def _():
        dx = mm(dab_ref[...], both_ref[...])
        rounded = dx.astype(bf16)
        out_ref[...] = rounded[:main]
        ext[jnp.minimum(step, 3)] = rounded[main:]
        part = jnp.sum(x_ref[...].astype(f32) * dx[:main] * s8[:, 0:1], axis=0, keepdims=True)
        part = part + jnp.sum(x2_ref[...].astype(f32) * dx[main:] * s2[:, 0:1], axis=0, keepdims=True)
        column = jnp.concatenate(
            [jnp.broadcast_to(part[:, j : j + MSG], (MSG, MSG)).T for j in range(0, quarter, MSG)], axis=0
        )
        dests = part_ref.shape[0] // SUB
        groups = quarter // dests // SUB
        column = column.reshape(dests, groups, SUB, MSG)
        lane = iota((dests, SUB, MSG), 2)
        spread = jnp.zeros((dests, SUB, MSG), f32)
        for g in range(groups):
            spread = jnp.where(lane == g, column[:, g], spread)
        part_ref[...] = spread.reshape(dests * SUB, MSG).astype(bf16)

    @pl.when(step == 4)
    def _():
        chunk = min(32, sources)
        n_rows, tail_rows = SUB * chunk, 2 * chunk
        row, col = iota((n_rows, 4 * tail_rows), 0), iota((n_rows, 4 * tail_rows), 1)
        pick = jnp.where(row == 4 * (col % tail_rows) + col // tail_rows, 1.0, 0.0).astype(bf16)
        for j in range(sources // chunk):
            quarters = [ext[q, j * tail_rows : (j + 1) * tail_rows, :] for q in range(4)]
            out_ref[j * n_rows : (j + 1) * n_rows, :] = mm(pick, jnp.concatenate(quarters, axis=0)).astype(bf16)


def dx_side(dab, both, r1, x2, scale, extra):
    sources = scale.shape[0]
    twice, width = both.shape
    quarter = width // 4
    main, total = sources * HI, 2 * sources

    def columns(n_rows):
        return pl.BlockSpec((n_rows, quarter), lambda i: (0, jnp.minimum(i, 3)))

    return pl.pallas_call(
        dx_kernel,
        grid=(5,),
        in_specs=[whole(dab.shape), columns(twice), columns(main), columns(total), whole(scale.shape)],
        out_specs=[
            pl.BlockSpec((main, quarter), lambda i: (0, i)),
            pl.BlockSpec((main // 4, MSG), lambda i: (jnp.minimum(i, 3), 0)),
        ],
        out_shape=[jax.ShapeDtypeStruct((main, width + extra), bf16), jax.ShapeDtypeStruct((main, MSG), bf16)],
        scratch_shapes=[pltpu.VMEM((4, total, quarter), bf16), pltpu.VMEM((main, MSG), f32), pltpu.VMEM((total, MSG), f32)],
        compiler_params=params(),
        cost_estimate=pl.CostEstimate(flops=2 * (main + total) * both.size, bytes_accessed=20_000_000, transcendentals=0),
    )(dab, both, r1, x2, scale)


def weights_kernel(x_ref, c_ref, x2_ref, c2_ref, act_ref, dab_ref, scale_ref, dwg_ref, dwu_ref, dwd_ref, act_s, dab_s):
    main = x_ref.shape[0]
    hid = act_ref.shape[1]
    tile = min(TILE, hid)

    @pl.when(pl.program_id(0) == 0)
    def _():
        table = scale_ref[...]
        column, tail_column = column_of(table.astype(f32)), tail_column_of(table)
        for source, target in ((act_ref, act_s), (dab_ref, dab_s)):
            target[:main] = (source[:main].astype(f32) * column).astype(bf16)
            target[main:] = (source[main:].astype(f32) * tail_column).astype(bf16)

    both = (mm_tn(x_ref[...], dab_s[:main]) + mm_tn(x2_ref[...], dab_s[main:])).astype(bf16)
    for j in range(hid // tile):
        dwg_ref[:, j * tile : (j + 1) * tile] = both[:, 2 * j * tile : (2 * j + 1) * tile]
        dwu_ref[:, j * tile : (j + 1) * tile] = both[:, (2 * j + 1) * tile : (2 * j + 2) * tile]
    dwd_ref[...] = (mm_tn(act_s[:main], c_ref[...]) + mm_tn(act_s[main:], c2_ref[...])).astype(bf16)


def weight_grads(r1, r2, x2, c2, act, dab, scale):
    total, hid = act.shape
    main, width = r1.shape[0], x2.shape[1]
    tile = min(256, width)
    steps = width // tile

    def columns(n_rows):
        return pl.BlockSpec((n_rows, tile), lambda i: (0, i))

    return pl.pallas_call(
        weights_kernel,
        grid=(steps,),
        in_specs=[columns(main), columns(main), columns(total - main), columns(total - main)]
        + [whole(act.shape), whole(dab.shape), whole(scale.shape)],
        out_specs=[pl.BlockSpec((tile, hid), lambda i: (i, 0)), pl.BlockSpec((tile, hid), lambda i: (i, 0)), columns(hid)],
        out_shape=[
            jax.ShapeDtypeStruct((width, hid), bf16),
            jax.ShapeDtypeStruct((width, hid), bf16),
            jax.ShapeDtypeStruct((hid, width), bf16),
        ],
        scratch_shapes=[pltpu.VMEM(act.shape, bf16), pltpu.VMEM(dab.shape, bf16)],
        compiler_params=params(),
        cost_estimate=pl.CostEstimate(flops=6 * total * width * hid, bytes_accessed=36_000_000, transcendentals=0),
    )(r1, r2, x2, c2, act, dab, scale)


def home_kernel(q_ref, slot_ref, gates_ref, normed_ref, part_ref, _, back_ref, dl_ref, gk_t_ref, router_part):
    step, last = pl.program_id(0), pl.num_programs(0) - 1
    experts = q_ref.shape[0]

    @pl.when(step == 0)
    def _():
        q_t = q_ref[...].T
        slot, gates = slot_ref[...], gates_ref[...]
        gated = jnp.zeros_like(gates)
        kept = jnp.zeros_like(gates)
        for s in range(10):
            here = slot == s
            gated = gated + jnp.where(here, q_t[s : s + 1, :], 0.0)
            kept = kept + jnp.where(here, q_t[10 + s : 11 + s, :], 0.0)
        rounded = gates.astype(bf16).astype(f32)
        gated = gated * jnp.where(rounded > 0.0, gates / jnp.where(rounded > 0.0, rounded, 1.0), 0.0)
        dsel = gated - gates * jnp.sum(gated, axis=1, keepdims=True)
        dl = dsel.astype(bf16)
        dl_ref[...] = dl
        gk_t_ref[...] = kept.T
        if experts < MSG:
            dl = jnp.concatenate([dl, jnp.zeros((dl.shape[0], MSG - experts), bf16)], axis=1)
        groups = router_part.shape[0]
        partial = mm_tn(normed_ref[...], dl).reshape(experts, groups, SUB, MSG)
        for g in range(groups):
            router_part[g] = partial[:, g].reshape(experts * SUB, MSG).astype(bf16)

    @pl.when(step < last)
    def _():
        back_ref[...] = router_part[jnp.minimum(step, router_part.shape[0] - 1)]

    @pl.when(step == last)
    def _():
        back_ref[...] = part_ref[...]


def home(q, slot, gates, normed, part, back):
    tokens, experts = slot.shape
    width = normed.shape[1]
    groups = width // experts // SUB
    first = (width + width // 4) // MSG
    return pl.pallas_call(
        home_kernel,
        grid=(groups + 1,),
        in_specs=[whole(q.shape), whole(slot.shape), whole(gates.shape), whole(normed.shape), whole(part.shape), pl.BlockSpec(memory_space=pl.ANY)],
        out_specs=[pl.BlockSpec((experts * SUB, MSG), lambda i: (0, first + i)), whole((tokens, experts)), whole((experts, tokens))],
        out_shape=[
            jax.ShapeDtypeStruct(back.shape, bf16),
            jax.ShapeDtypeStruct((tokens, experts), bf16),
            jax.ShapeDtypeStruct((experts, tokens), f32),
        ],
        scratch_shapes=[pltpu.VMEM((groups, experts * SUB, MSG), bf16)],
        input_output_aliases={5: 0},
        compiler_params=params(),
        cost_estimate=pl.CostEstimate(flops=2 * tokens * MSG * width, bytes_accessed=2_500_000, transcendentals=0),
    )(q, slot, gates, normed, part, back)


def sums_kernel(*refs):
    *parts, gain_ref, router_ref, gain_rows_ref, target_ref, out_ref = refs
    copies, n_rows, _ = out_ref.shape
    target = target_ref[...]
    row = iota(target.shape, 0)
    gain_parts = jnp.sum(gain_ref[...].astype(f32).reshape(copies, SUB, MSG), axis=0)
    pieces = []
    placed = jnp.zeros(target.shape, f32)
    for g, ref in enumerate(parts):
        piece = jnp.sum(ref[...].astype(f32).reshape(copies, SUB, MSG), axis=0)
        pieces.append(piece)
        own = slice(g * SUB, (g + 1) * SUB)
        value = gain_parts[:, g : g + 1] + jnp.sum(router_ref[own] * piece, axis=1, keepdims=True)
        placed = jnp.where(target == g * SUB + row, value / gain_rows_ref[own], placed)
    message = jnp.concatenate(pieces + [placed], axis=0)
    out_ref[...] = jnp.broadcast_to(message[None], out_ref.shape).astype(bf16)


def sums(rd, router_rows, gain_rows, target, experts, width):
    groups = width // experts // SUB
    first = (width + width // 4) // MSG
    block = (experts * SUB, MSG)
    specs = [pl.BlockSpec(block, functools.partial(lambda g, i: (0, first + g), g)) for g in range(groups + 1)]
    return pl.pallas_call(
        sums_kernel,
        grid=(1,),
        in_specs=specs + [whole(router_rows.shape), whole(gain_rows.shape), whole(target.shape)],
        out_specs=whole((experts, (groups + 1) * SUB, MSG)),
        out_shape=jax.ShapeDtypeStruct((experts, (groups + 1) * SUB, MSG), bf16),
        compiler_params=params(),
        cost_estimate=pl.CostEstimate(flops=experts * SUB * MSG * 8, bytes_accessed=2_000_000, transcendentals=0),
    )(*[rd] * (groups + 1), router_rows, gain_rows, target)


def final_kernel(dx_ref, ext_ref, slot_t_ref, gk_t_ref, dl_ref, router_ref, gain_ref, hid_ref, cot_ref, dh_ref, total):
    step, last = pl.program_id(0), pl.num_programs(0) - 1
    chunk, tokens = slot_t_ref.shape
    n_rows = chunk * SUB
    quarter = ext_ref.shape[1]
    slot, gk = slot_t_ref[...][:, None, :], gk_t_ref[...][:, None, :]
    which = iota((chunk, SUB, tokens), 1)

    def weights(mask):
        return jnp.where(mask, gk, 0.0).reshape(n_rows, tokens).astype(bf16)

    @pl.when(step == 0)
    def _():
        total[...] = mm_nt(dl_ref[...], router_ref[...])

    total[...] += mm_tn(weights(slot == which.astype(f32)), dx_ref[...])
    in_tail = slot == (HI + which // 4).astype(f32)
    for j in range(4):
        total[:, j * quarter : (j + 1) * quarter] += mm_tn(weights(in_tail & (which % 4 == j)), ext_ref[...])

    @pl.when(step == last)
    def _():
        h = hid_ref[...].astype(f32)
        scale = lax.rsqrt(jnp.mean(h * h, axis=1, keepdims=True) + norm_eps)
        gained = gain_ref[...] * total[...]
        mean = jnp.mean(gained * h, axis=1, keepdims=True)
        dh_ref[...] = (cot_ref[...].astype(f32) + scale * gained - h * (scale * scale * scale) * mean).astype(bf16)


def final(rd, slot_t, gk_t, dl, router, gain, hidden, cotangent):
    experts, tokens = slot_t.shape
    width = hidden.shape[1]
    chunk = min(32, experts)
    steps = experts // chunk
    return pl.pallas_call(
        final_kernel,
        grid=(steps,),
        in_specs=[
            pl.BlockSpec((chunk * SUB, width), lambda i: (i, 0)),
            pl.BlockSpec((chunk * SUB, width // 4), lambda i: (i, 4)),
            pl.BlockSpec((chunk, tokens), lambda i: (i, 0)),
            pl.BlockSpec((chunk, tokens), lambda i: (i, 0)),
            whole(dl.shape),
            whole(router.shape),
            whole((1, width)),
            whole((tokens, width)),
            whole((tokens, width)),
        ],
        out_specs=whole((tokens, width)),
        out_shape=jax.ShapeDtypeStruct((tokens, width), bf16),
        scratch_shapes=[pltpu.VMEM((tokens, width), f32)],
        compiler_params=params(),
        cost_estimate=pl.CostEstimate(flops=4 * experts * SUB * tokens * width, bytes_accessed=9_000_000, transcendentals=tokens),
    )(rd, rd, slot_t, gk_t, dl, router, gain, hidden, cotangent)


def place_kernel(sums_ref, router_ref, gain_ref):
    experts, n_rows, _ = sums_ref.shape
    rows_each = n_rows - SUB
    received = sums_ref[...].astype(f32)
    router_ref[...] = received[:, :rows_each].reshape(experts * rows_each, MSG)[:, : router_ref.shape[1]]
    gain_ref[...] = jnp.sum(received[:, rows_each:].reshape(gain_ref.shape[0], -1, MSG), axis=1)


def place(received, width, experts):
    return pl.pallas_call(
        place_kernel,
        out_shape=[jax.ShapeDtypeStruct((width, experts), f32), jax.ShapeDtypeStruct((width // MSG, MSG), f32)],
        compiler_params=params(16),
        cost_estimate=pl.CostEstimate(flops=received.size, bytes_accessed=2_000_000, transcendentals=0),
    )(received)


def on_device(hidden, cotangent, norm_gain, router, w_gate, w_up, w_down, expert_ids):
    tokens, width = hidden.shape
    top = expert_ids.shape[1]
    experts = router.shape[1]
    quarter = width // 4
    limit = tokens * top
    gain = norm_gain.reshape(1, width)
    wg, wu, wd = w_gate[0], w_up[0], w_down[0]
    own = width // experts
    extra = quarter + (own // SUB + 1) * MSG

    me = lax.axis_index(AXES)
    router_rows = lax.dynamic_slice_in_dim(router, me * own, own, 0).astype(f32)
    router_rows = jnp.pad(router_rows, ((0, 0), (0, MSG - experts)))
    gain_rows = jnp.broadcast_to(lax.dynamic_slice_in_dim(norm_gain, me * own, own, 0)[:, None], (own, MSG))
    target = lax.broadcasted_iota(jnp.int32, (SUB, MSG), 1) - (me % (MSG // own)) * own

    s1, normed, slot, slot_t = front(hidden, gain, expert_ids.T, experts)
    r1 = exchange(s1.reshape(experts, HI, width + quarter)).reshape(experts * HI, width + quarter)
    gates, s2 = second(normed, cotangent, slot, slot_t, router)
    both, wd_t = turn(wg, wu, wd)
    r2 = exchange(s2.reshape(experts, SUB, width + quarter)).reshape(experts * SUB, width + quarter)
    act, fa, fb, x2 = x_side(r1, wg, wu)
    dab, c2, q_msg, scale = c_side(r2, wd_t, act, fa, fb, limit)
    q_home = exchange(q_msg.reshape(experts, 1, MSG)).reshape(experts, MSG)
    back, part = dx_side(dab, both, r1, x2, scale, extra)
    back, dl, gk_t = home(q_home, slot, gates, normed, part, back)
    scale, dl = lax.optimization_barrier((scale, dl))
    d_wgate, d_wup, d_wdown = weight_grads(r1, r2, x2, c2, act, dab, scale)
    rd = exchange(back.reshape(experts, HI, width + extra)).reshape(experts * HI, width + extra)
    d_wgate, gain_rows, router_rows, target = lax.optimization_barrier((d_wgate, gain_rows, router_rows, target))
    message = sums(rd, router_rows, gain_rows, target, experts, width)
    received = exchange(message)
    d_hidden = final(rd, slot_t, gk_t, dl, router, gain, hidden, cotangent)
    d_router, d_gain = place(received, width, experts)
    return (d_hidden, d_gain.reshape(width), d_router, d_wgate[None], d_wup[None], d_wdown[None])


def solution(mesh):
    rows_spec, stack_spec = P(AXES, None), P(AXES, None, None)
    in_specs = (rows_spec, rows_spec, P(), P(), stack_spec, stack_spec, stack_spec, rows_spec)
    out_specs = (rows_spec, P(), P(), stack_spec, stack_spec, stack_spec)
    return jax.shard_map(on_device, mesh=mesh, in_specs=in_specs, out_specs=out_specs, check_vma=False)
```
